32 devices in a mesh: sp: 16 (over z, y, core), gz: 2 (over x).
Axes of the slice: x: 2, y: 2, z: 4, core: 2. Of those that a mesh axis runs over, the one named last changes fastest.
Arguments:
- volume: bfloat16 [128, 32, 8, 256], P(None, 'sp', 'gz'), may hold values from -6 to 6
- weight: bfloat16 [3, 3, 3, 64, 128], replicated, may hold values from -0.15625 to 0.15625
- cotangent: bfloat16 [128, 16, 4, 128], P(None, 'sp', 'gz'), may hold values from -6 to 6
Outputs:
- layer_out: bfloat16 [128, 16, 4, 128], P(None, 'sp', 'gz')
- volume_grad: bfloat16 [128, 32, 8, 256], P(None, 'sp', 'gz')
- kernel_grad: float32 [3, 3, 3, 64, 128], replicated
The draws below stay inside these ranges and needn't reach their ends.
All inputs are finite; a program needn't handle non-finite values.
Results may differ from the reference program's by a relative error of at most 0.001.
Values may be sent and summed in bfloat16 or wider, within the bound.
No kernel may reach another device: no remote copies, remote signals or barrier semaphores. Data moves between devices by JAX's collectives and lax.ppermute only.
A program may use at most 64 MiB of HBM per device.

```python
import math
import jax
import jax.numpy as jnp
from jax import lax

CIN = 128
COUT = 128
GROUPS = 2
NX = 256
GW = 64
NZ = 32
NY = 8


def levels(own_key, shape, cuts, smallest, top_value):
    level = 1.0
    for axis_at, shards_of in cuts:
        heights = jax.random.uniform(jax.random.fold_in(jax.random.fold_in(own_key, 6), axis_at), (shards_of,), jnp.float32, smallest / len(cuts), top_value / len(cuts))
        level = level * jnp.repeat(jnp.exp(heights), shape[axis_at] // shards_of).reshape((-1,) + (1,) * (len(shape) - 1 - axis_at))
    return level


def noise(rng, extent, deviation, bound, pieces=(), dtype=jnp.bfloat16):
    values = jax.random.normal(rng, extent, jnp.float32) * deviation
    if len(pieces) > 0:
        values = levels(rng, extent, pieces, -0.22, 0.18) * values
    return jnp.clip(values, min=-bound, max=bound).astype(dtype)


def setup_inputs(seed: int = 0) -> dict:
    arg_keys = jax.random.split(jax.random.key(seed), 4)
    return {
        "volume": noise(arg_keys[0], (CIN, NZ, NY, NX), 1.0, 6.0, ((1, 16), (2, 2))),
        "weight": noise(arg_keys[1], (3, 3, 3, GW, COUT), (27 * GW) ** -0.5, 0.15625),
        "cotangent": noise(arg_keys[2], (COUT, NZ // 2, NY // 2, NX // 2), 1.0, 6.0, ((1, 16), (2, 2))),
    }


def forward(as_float, kernel):
    return lax.conv_general_dilated(as_float[None], kernel, (2, 2, 2), ((1, 1), (1, 1), (1, 1)), dimension_numbers=('NCDHW', 'DHWIO', 'NCDHW'), feature_group_count=GROUPS, precision=lax.Precision.HIGHEST)[0]

def reference(volume, weight, cotangent):
    as_float = volume.astype(jnp.float32)
    kernel = weight.astype(jnp.float32)
    upstream = cotangent.astype(jnp.float32)
    layer_out, pullback = jax.vjp(forward, as_float, kernel)
    vol_grad, weight_grad = pullback(upstream)
    grad_scale = 1.0 / math.sqrt(NZ * NY * NX / 8)
    return (layer_out.astype(jnp.bfloat16), vol_grad.astype(jnp.bfloat16), (weight_grad * grad_scale).astype(jnp.float32))
```

```python
import functools
import math

import jax
import jax.numpy as jnp
from jax import lax
from jax.experimental import pallas as pl
from jax.experimental.pallas import tpu as pltpu
from jax.sharding import PartitionSpec as P

GROUPS = 2
BF = jnp.bfloat16
F32 = jnp.float32
F16 = jnp.float16


def dot(left, right, dims=((1,), (0,))):
    return lax.dot_general(left, right, (dims, ((), ())), preferred_element_type=F32)


def exact(left, right):
    return dot(left, right).astype(BF)


def ones_where(shape, condition):
    row = lax.broadcasted_iota(jnp.int32, shape, 0)
    col = lax.broadcasted_iota(jnp.int32, shape, 1)
    return jnp.where(condition(row, col), 1.0, 0.0).astype(BF)


def rows_grouped(block, inner):
    size = block * inner
    return ones_where((size, size), lambda row, col: col == (row % block) * inner + row // block)


def rows_interleaved(block, inner):
    size = block * inner
    return ones_where((size, size), lambda row, col: row == (col % block) * inner + col // block)


def taps_of(parity):
    return (1,) if parity == 0 else (0, 2)


def kernel_grad_body(
    core_ref, vol_ref, own_ref, up_z_ref, up_y_ref, up_c_ref,
    planes_ref, cots_ref, keep_ref, send_ref, class_ref, shift_ref, grad_ref,
):
    channels, z_cells, y_cells, x_cells = vol_ref.shape
    out_x = x_cells // 2
    out_y = y_cells // 2
    lines = z_cells * y_cells
    width = channels // GROUPS

    by_row = rows_grouped(channels, out_y)
    moved = ones_where(
        (out_x, 2 * out_x),
        lambda row, col: row == jnp.where(col < out_x, col, col - out_x + 1),
    )
    for plane, (here, above) in enumerate(((own_ref, up_y_ref), (up_z_ref, up_c_ref))):
        for source, first, count in ((here, 0, out_y), (above, out_y, 1)):
            rows = exact(by_row, source[...].reshape(channels * out_y, out_x))
            both = exact(rows[: count * channels], moved)
            for k in range(count):
                cots_ref[plane * (out_y + 1) + first + k] = both[k * channels : (k + 1) * channels]

    block = 256 // lines
    by_line = rows_grouped(block, lines)
    halves = ones_where(
        (x_cells, x_cells),
        lambda row, col: row == jnp.where(col < out_x, 2 * col, 2 * (col - out_x) + 1),
    )
    for at in range(0, channels, block):
        rows = vol_ref[at : at + block].reshape(block * lines, x_cells)
        rows = exact(exact(by_line, rows), halves)
        for k in range(lines):
            planes_ref[k, at : at + block, :] = rows[k * block : (k + 1) * block]

    for z in range(z_cells):
        for y_par in range(2):
            for x_par in range(2):
                for y in range(out_y):
                    class_ref[(z * 2 + y_par) * 2 + x_par, :, y * out_x : (y + 1) * out_x] = planes_ref[
                        z * y_cells + 2 * y + y_par, :, x_par * out_x : (x_par + 1) * out_x
                    ]
    for plane in range(2):
        for off in range(2):
            for step in range(2):
                for y in range(out_y):
                    shift_ref[(plane * 2 + off) * 2 + step, :, y * out_x : (y + 1) * out_x] = cots_ref[
                        plane * (out_y + 1) + off + y, :, step * out_x : (step + 1) * out_x
                    ]

    first_half = lax.broadcasted_iota(jnp.int32, (width, channels), 1) < width
    for a in range(3):
        for b in range(3):
            for c in range(3):
                which = ((a != 1) * 2 + (b != 1)) * 2 + (c != 1)
                cot = ((a == 0) * 2 + (b == 0)) * 2 + (c == 0)
                full = dot(class_ref[which], shift_ref[cot], ((1,), (1,)))
                tap = (a * 3 + b) * 3 + c
                grad_ref[tap * width : (tap + 1) * width] = jnp.where(
                    first_half, full[:width], full[width:]
                )

    parts, padded, _ = keep_ref.shape
    half = grad_ref.shape[0] // 2
    each = half // parts
    top = jnp.maximum(jnp.max(jnp.abs(grad_ref[...])), 1e-30)
    level = jnp.floor(jnp.log2(jnp.full((padded - each, channels), top, F32))) - 14.0
    low = core_ref[0] == 0
    for k in range(parts):
        here = grad_ref[k * each : (k + 1) * each]
        there = grad_ref[half + k * each : half + (k + 1) * each]
        keep_ref[k, :each] = jnp.where(low, here, there)
        send_ref[k, :each] = jnp.where(low, there, here)
        keep_ref[k, each:] = level
        send_ref[k, each:] = level


def outputs_body(
    planes_ref, from_z_ref, from_y_ref, from_c_ref, cots_ref, weight_ref,
    out_ref, grad_ref, spread_ref, patch_ref, shift_ref, lines_ref,
):
    lines, channels, x_cells = planes_ref.shape
    y_cells = from_z_ref.shape[0]
    z_cells = lines // y_cells
    out_x = x_cells // 2
    out_y = y_cells // 2
    width = channels // GROUPS

    first_half = lax.broadcasted_iota(jnp.int32, (width, channels), 1) < width
    for tap in range(27):
        part = weight_ref[tap]
        zero = jnp.zeros_like(part)
        spread_ref[tap * channels : tap * channels + width] = jnp.where(first_half, part, zero)
        spread_ref[tap * channels + width : (tap + 1) * channels] = jnp.where(first_half, zero, part)

    moved = ones_where((out_x, out_x), lambda row, col: row == col - 1)

    def line(a, row):
        if row == 0:
            return from_c_ref[0] if a == 0 else from_y_ref[a - 1]
        return from_z_ref[row - 1] if a == 0 else planes_ref[(a - 1) * y_cells + row - 1]

    for a in range(3):
        for row in range(2 * out_y + 1):
            cells = line(a, row)
            even, odd = cells[:, :out_x], cells[:, out_x:]
            pieces = (exact(odd, moved), even, odd)
            for b in range(3):
                y = (row - b) // 2
                if (row - b) % 2 == 0 and 0 <= y < out_y:
                    for c in range(3):
                        tap = (a * 3 + b) * 3 + c
                        patch_ref[
                            tap * channels : (tap + 1) * channels, y * out_x : (y + 1) * out_x
                        ] = pieces[c]
    result = dot(spread_ref[...], patch_ref[...], ((0,), (0,))).astype(BF)
    stacked = jnp.concatenate(
        [result[:, y * out_x : (y + 1) * out_x] for y in range(out_y)], axis=0
    )
    out_ref[...] = exact(rows_interleaved(channels, out_y), stacked).reshape(out_ref.shape)

    for plane in range(2):
        for off in range(2):
            for step in range(2):
                for y in range(out_y):
                    shift_ref[(plane * 2 + off) * 2 + step, :, y * out_x : (y + 1) * out_x] = cots_ref[
                        plane * (out_y + 1) + off + y, :, step * out_x : (step + 1) * out_x
                    ]
    for z in range(z_cells):
        for y_par in range(2):
            for x_par in range(2):
                total = jnp.zeros((channels, out_y * out_x), F32)
                for a in taps_of(z):
                    for b in taps_of(y_par):
                        for c in taps_of(x_par):
                            tap = (a * 3 + b) * 3 + c
                            cot = ((a == 0) * 2 + (b == 0)) * 2 + (c == 0)
                            total += dot(
                                spread_ref[tap * channels : (tap + 1) * channels], shift_ref[cot]
                            )
                total = total.astype(BF)
                for y in range(out_y):
                    lines_ref[
                        z * y_cells + 2 * y + y_par, :, x_par * out_x : (x_par + 1) * out_x
                    ] = total[:, y * out_x : (y + 1) * out_x]
    block = 256 // lines
    by_cell = rows_interleaved(block, lines)
    joined = ones_where(
        (x_cells, x_cells),
        lambda row, col: col == jnp.where(row < out_x, 2 * row, 2 * (row - out_x) + 1),
    )
    for at in range(0, channels, block):
        rows = jnp.concatenate([lines_ref[k, at : at + block, :] for k in range(lines)], axis=0)
        rows = exact(by_cell, exact(rows, joined))
        grad_ref[at : at + block] = rows.reshape(block, z_cells, y_cells, x_cells)


def shifted(array, by_z, by_y):
    size_z, size_y = lax.axis_size("sp"), lax.axis_size("gz")
    pairs = []
    for z in range(size_z):
        for y in range(size_y):
            to_z, to_y = z + by_z, y + by_y
            if 0 <= to_z < size_z and 0 <= to_y < size_y:
                pairs.append((z * size_y + y, to_z * size_y + to_y))
    return lax.ppermute(array, ("sp", "gz"), pairs)


def swapped(array, flip):
    return lax.ppermute(array, "sp", [(i, i ^ flip) for i in range(lax.axis_size("sp"))])


def coded(values, level, each):
    row = lax.broadcasted_iota(jnp.int32, values.shape, values.ndim - 2)
    return jnp.where(row < each, values * jnp.exp2(-level), level).astype(F16)


def summed(keep, got, each, parts):
    size_z, size_y = lax.axis_size("sp"), lax.axis_size("gz")
    quads = size_z // 4
    level = jnp.maximum(keep[:, each : each + 1], got[:, each : each + 1]) + 1.0
    message = coded(keep + got, level, each)
    groups = [
        [(q * 4 + y * 2 + core) * size_y + g for y in range(2) for g in range(size_y)]
        for q in range(quads)
        for core in range(2)
    ]

    def exchange(array):
        return lax.all_to_all(
            array, ("sp", "gz"), 0, 0, tiled=True, axis_index_groups=groups
        )

    received = exchange(message).astype(F32)
    levels = received[:, each : each + 1]
    level = jnp.max(levels, axis=0) + math.ceil(math.log2(parts))
    message = coded(jnp.sum(received * jnp.exp2(levels), axis=0), level, each)
    terms = [message] + [swapped(message, 4 * k) for k in range(1, quads)]
    terms = [(t.astype(F32), t[each : each + 1].astype(F32)) for t in terms]
    terms = [(t * jnp.exp2(level), level) for t, level in terms]
    while len(terms) > 1:
        terms = [
            (left[0] + right[0], jnp.maximum(left[1], right[1]) + 1.0)
            for left, right in zip(terms[::2], terms[1::2])
        ]
    message = coded(terms[0][0], terms[0][1], each)
    message = jnp.broadcast_to(message[None], (parts,) + message.shape)
    return exchange(message)


def per_device(volume, weight, cotangent):
    channels, z_cells, y_cells, x_cells = volume.shape
    slabs, pencils = lax.axis_size("sp"), lax.axis_size("gz")
    width = channels // GROUPS
    out_channels = weight.shape[4]
    out_z, out_y, out_x = cotangent.shape[1:]
    lines = z_cells * y_cells
    out_cells = slabs * pencils * out_z * out_y * out_x
    parts = 2 * pencils
    rows = 27 * width
    each = rows // 2 // parts
    padded = (each + 8) // 8 * 8
    core = lax.axis_index("sp") % 2

    up_z = shifted(cotangent, -1, 0)
    up_y = shifted(cotangent, 0, -1)
    up_c = shifted(cotangent, -1, -1)
    vmem = pl.BlockSpec(memory_space=pltpu.VMEM)
    share = jax.ShapeDtypeStruct((parts, padded, out_channels), F32)
    planes, cots, keep, send = pl.pallas_call(
        kernel_grad_body,
        out_shape=(
            jax.ShapeDtypeStruct((lines, channels, x_cells), BF),
            jax.ShapeDtypeStruct((2 * (out_y + 1), channels, x_cells), BF),
            share,
            share,
        ),
        in_specs=[pl.BlockSpec(memory_space=pltpu.SMEM)] + [vmem] * 5,
        out_specs=(vmem,) * 4,
        scratch_shapes=[
            pltpu.VMEM((8, channels, out_y * out_x), BF),
            pltpu.VMEM((8, channels, out_y * out_x), BF),
            pltpu.VMEM((rows, out_channels), F32),
        ],
        compiler_params=pltpu.CompilerParams(vmem_limit_bytes=32 * 1024 * 1024),
        cost_estimate=pl.CostEstimate(flops=1_000_000_000, bytes_accessed=4_000_000, transcendentals=0),
    )(core.reshape(1), volume, cotangent, up_z, up_y, up_c)

    got = swapped(send, 1)
    mine = summed(keep, got, each, parts)
    other = swapped(mine, 1)

    def plain(coded_half):
        values = coded_half.astype(F32)
        values = values * jnp.exp2(values[:, each : each + 1]) * (1.0 / math.sqrt(out_cells))
        return values[:, :each].reshape(rows // 2, out_channels)

    mine, other = plain(mine), plain(other)
    kernel_grad = jnp.concatenate(
        [jnp.where(core == 0, mine, other), jnp.where(core == 0, other, mine)], axis=0
    ).reshape(weight.shape)

    last = planes.reshape(z_cells, y_cells, channels, x_cells)
    from_z = shifted(last[-1], 1, 0)
    from_y = shifted(last[:, -1], 0, 1)
    from_c = shifted(last[-1, -1:], 1, 1)
    output, volume_grad = pl.pallas_call(
        outputs_body,
        out_shape=(
            jax.ShapeDtypeStruct(cotangent.shape, BF),
            jax.ShapeDtypeStruct(volume.shape, BF),
        ),
        in_specs=[vmem] * 6,
        out_specs=(vmem,) * 2,
        scratch_shapes=[
            pltpu.VMEM((27 * channels, out_channels), BF),
            pltpu.VMEM((27 * channels, out_y * out_x), BF),
            pltpu.VMEM((8, channels, out_y * out_x), BF),
            pltpu.VMEM((lines, channels, x_cells), BF),
        ],
        compiler_params=pltpu.CompilerParams(vmem_limit_bytes=32 * 1024 * 1024),
        cost_estimate=pl.CostEstimate(flops=2_000_000_000, bytes_accessed=4_000_000, transcendentals=0),
    )(planes, from_z, from_y, from_c, cots, weight.reshape(27, width, out_channels))
    return (output, volume_grad, kernel_grad)


def solution(mesh):
    in_specs = (P(None, "sp", "gz", None), P(), P(None, "sp", "gz", None))
    out_specs = (P(None, "sp", "gz", None), P(None, "sp", "gz", None), P())
    return jax.shard_map(
        per_device, mesh=mesh, in_specs=in_specs, out_specs=out_specs, check_vma=False
    )
```

```python
import functools
import math

import jax
import jax.numpy as jnp
from jax import lax
from jax.experimental import pallas as pl
from jax.experimental.pallas import tpu as pltpu
from jax.sharding import PartitionSpec as P

GROUPS = 2
BF = jnp.bfloat16
F32 = jnp.float32
F16 = jnp.float16


def dot(left, right, dims=((1,), (0,))):
    return lax.dot_general(left, right, (dims, ((), ())), preferred_element_type=F32)


def exact(left, right):
    return dot(left, right).astype(BF)


def ones_where(shape, condition):
    row = lax.broadcasted_iota(jnp.int32, shape, 0)
    col = lax.broadcasted_iota(jnp.int32, shape, 1)
    return jnp.where(condition(row, col), 1.0, 0.0).astype(BF)


def rows_grouped(block, inner):
    size = block * inner
    return ones_where((size, size), lambda row, col: col == (row % block) * inner + row // block)


def rows_interleaved(block, inner):
    size = block * inner
    return ones_where((size, size), lambda row, col: row == (col % block) * inner + col // block)


def taps_of(parity):
    return (1,) if parity == 0 else (0, 2)


def lay_out_body(vol_ref, own_ref, planes_ref, cots_ref):
    channels, z_cells, y_cells, x_cells = vol_ref.shape
    out_x = x_cells // 2
    lines = z_cells * y_cells
    block = 256 // lines
    by_line = rows_grouped(block, lines)
    halves = ones_where(
        (x_cells, x_cells),
        lambda row, col: row == jnp.where(col < out_x, 2 * col, 2 * (col - out_x) + 1),
    )
    for at in range(0, channels, block):
        rows = vol_ref[at : at + block].reshape(block * lines, x_cells)
        rows = exact(exact(by_line, rows), halves)
        for k in range(lines):
            planes_ref[k, at : at + block, :] = rows[k * block : (k + 1) * block]
    lay_out_cotangent(own_ref, cots_ref, 0, cots_ref.shape[0])


def lay_out_cotangent(source_ref, cots_ref, first, count):
    channels, _, out_y, out_x = source_ref.shape
    by_row = rows_grouped(channels, out_y)
    moved = ones_where(
        (out_x, 2 * out_x),
        lambda row, col: row == jnp.where(col < out_x, col, col - out_x + 1),
    )
    rows = exact(by_row[: count * channels], source_ref[...].reshape(channels * out_y, out_x))
    both = exact(rows, moved)
    for k in range(count):
        cots_ref[first + k] = both[k * channels : (k + 1) * channels]


def kernel_grad_body(
    place_ref, planes_ref, own_ref, up_z_ref, up_y_ref, up_c_ref,
    cots_ref, keep_ref, send_ref, class_ref, shift_ref, grad_ref,
):
    lines, channels, x_cells = planes_ref.shape
    out_x = x_cells // 2
    out_y = own_ref.shape[0]
    y_cells = 2 * out_y
    z_cells = lines // y_cells
    width = channels // GROUPS

    cots_ref[:out_y] = own_ref[...]
    lay_out_cotangent(up_y_ref, cots_ref, out_y, 1)
    lay_out_cotangent(up_z_ref, cots_ref, out_y + 1, out_y)
    lay_out_cotangent(up_c_ref, cots_ref, 2 * out_y + 1, 1)

    for z in range(z_cells):
        for y_par in range(2):
            for x_par in range(2):
                for y in range(out_y):
                    class_ref[(z * 2 + y_par) * 2 + x_par, :, y * out_x : (y + 1) * out_x] = planes_ref[
                        z * y_cells + 2 * y + y_par, :, x_par * out_x : (x_par + 1) * out_x
                    ]
    pair_rows(cots_ref, shift_ref)

    first_half = lax.broadcasted_iota(jnp.int32, (width, channels), 1) < width
    for a in range(3):
        for b in range(3):
            for c in range(3):
                which = ((a != 1) * 2 + (b != 1)) * 2 + (c != 1)
                cot = ((a == 0) * 2 + (b == 0)) * 2 + (c == 0)
                full = dot(class_ref[which], shift_ref[cot], ((1,), (1,)))
                tap = (a * 3 + b) * 3 + c
                grad_ref[tap * width : (tap + 1) * width] = jnp.where(
                    first_half, full[:width], full[width:]
                )

    parts, padded, _ = keep_ref.shape
    half = grad_ref.shape[0] // 2
    each = half // parts
    top = jnp.maximum(jnp.max(jnp.abs(grad_ref[...])), 1e-30)
    level = jnp.floor(jnp.log2(jnp.full((padded - each, channels), top, F32))) - 14.0
    low = place_ref[0] == 0
    for part in range(parts):
        slot = place_ref[1] ^ part
        here = grad_ref[part * each : (part + 1) * each]
        there = grad_ref[half + part * each : half + (part + 1) * each]
        keep_ref[slot, :each] = jnp.where(low, here, there)
        send_ref[slot, :each] = jnp.where(low, there, here)
        keep_ref[slot, each:] = level
        send_ref[slot, each:] = level


def pair_rows(cots_ref, shift_ref):
    out_y = cots_ref.shape[0] // 2 - 1
    out_x = cots_ref.shape[2] // 2
    for plane in range(2):
        for off in range(2):
            for step in range(2):
                for y in range(out_y):
                    shift_ref[(plane * 2 + off) * 2 + step, :, y * out_x : (y + 1) * out_x] = cots_ref[
                        plane * (out_y + 1) + off + y, :, step * out_x : (step + 1) * out_x
                    ]


def spread_groups(weight_ref, spread_ref):
    _, width, channels = weight_ref.shape
    first_half = lax.broadcasted_iota(jnp.int32, (width, channels), 1) < width
    for tap in range(27):
        part = weight_ref[tap]
        zero = jnp.zeros_like(part)
        spread_ref[tap * channels : tap * channels + width] = jnp.where(first_half, part, zero)
        spread_ref[tap * channels + width : (tap + 1) * channels] = jnp.where(first_half, zero, part)


def forward_body(
    planes_ref, from_z_ref, from_y_ref, weight_ref, out_ref, spread_ref, patch_ref,
):
    lines, channels, x_cells = planes_ref.shape
    y_cells = from_z_ref.shape[0]
    out_x = x_cells // 2
    out_y = y_cells // 2
    spread_groups(weight_ref, spread_ref)

    moved = ones_where((out_x, out_x), lambda row, col: row == col - 1)

    def line(a, row):
        if row == 0:
            return from_y_ref[a]
        return from_z_ref[row - 1] if a == 0 else planes_ref[(a - 1) * y_cells + row - 1]

    for a in range(3):
        for row in range(2 * out_y + 1):
            cells = line(a, row)
            even, odd = cells[:, :out_x], cells[:, out_x:]
            pieces = (exact(odd, moved), even, odd)
            for b in range(3):
                y = (row - b) // 2
                if (row - b) % 2 == 0 and 0 <= y < out_y:
                    for c in range(3):
                        tap = (a * 3 + b) * 3 + c
                        patch_ref[
                            tap * channels : (tap + 1) * channels, y * out_x : (y + 1) * out_x
                        ] = pieces[c]
    result = dot(spread_ref[...], patch_ref[...], ((0,), (0,))).astype(BF)
    stacked = jnp.concatenate(
        [result[:, y * out_x : (y + 1) * out_x] for y in range(out_y)], axis=0
    )
    out_ref[...] = exact(rows_interleaved(channels, out_y), stacked).reshape(out_ref.shape)


def backward_body(cots_ref, weight_ref, grad_ref, spread_ref, shift_ref, lines_ref):
    channels, z_cells, y_cells, x_cells = grad_ref.shape
    lines = z_cells * y_cells
    out_x = x_cells // 2
    out_y = y_cells // 2
    spread_groups(weight_ref, spread_ref)
    pair_rows(cots_ref, shift_ref)

    for z in range(z_cells):
        for y_par in range(2):
            for x_par in range(2):
                total = jnp.zeros((channels, out_y * out_x), F32)
                for a in taps_of(z):
                    for b in taps_of(y_par):
                        for c in taps_of(x_par):
                            tap = (a * 3 + b) * 3 + c
                            cot = ((a == 0) * 2 + (b == 0)) * 2 + (c == 0)
                            total += dot(
                                spread_ref[tap * channels : (tap + 1) * channels], shift_ref[cot]
                            )
                total = total.astype(BF)
                for y in range(out_y):
                    lines_ref[
                        z * y_cells + 2 * y + y_par, :, x_par * out_x : (x_par + 1) * out_x
                    ] = total[:, y * out_x : (y + 1) * out_x]
    block = 256 // lines
    by_cell = rows_interleaved(block, lines)
    joined = ones_where(
        (x_cells, x_cells),
        lambda row, col: col == jnp.where(row < out_x, 2 * row, 2 * (row - out_x) + 1),
    )
    for at in range(0, channels, block):
        rows = jnp.concatenate([lines_ref[k, at : at + block, :] for k in range(lines)], axis=0)
        rows = exact(by_cell, exact(rows, joined))
        grad_ref[at : at + block] = rows.reshape(block, z_cells, y_cells, x_cells)


def assemble_body(scale, parts, each, place_ref, *refs):
    slots, out_ref, held_ref = refs[:-2], refs[-2], refs[-1]
    half = parts * each
    for k, slot_ref in enumerate(slots):
        held_ref[k] = slot_ref[:each] * (jnp.exp2(slot_ref[each : each + 1]) * scale)
    for side in range(2):
        for part in range(parts):
            slot = (place_ref[0] ^ side) * parts + (place_ref[1] ^ part)
            at = side * half + part * each
            out_ref[at : at + each] = held_ref[slot]


def shifted(array, by_z, by_y):
    size_z, size_y = lax.axis_size("sp"), lax.axis_size("gz")
    pairs = []
    for z in range(size_z):
        for y in range(size_y):
            to_z, to_y = z + by_z, y + by_y
            if 0 <= to_z < size_z and 0 <= to_y < size_y:
                pairs.append((z * size_y + y, to_z * size_y + to_y))
    return lax.ppermute(array, ("sp", "gz"), pairs)


def swapped(array, flip):
    return lax.ppermute(array, "sp", [(i, i ^ flip) for i in range(lax.axis_size("sp"))])


def swapped_in_plane(array, flip):
    size_z, size_y = lax.axis_size("sp"), lax.axis_size("gz")
    pairs = []
    for z in range(size_z):
        for y in range(size_y):
            to = ((z // 2 % 2) * size_y + y) ^ flip
            to_z = z // 4 * 4 + to // size_y * 2 + z % 2
            pairs.append((z * size_y + y, to_z * size_y + to % size_y))
    return lax.ppermute(array, ("sp", "gz"), pairs)


def coded(values, level, each):
    row = lax.broadcasted_iota(jnp.int32, values.shape, 0)
    return jnp.where(row < each, values * jnp.exp2(-level), level).astype(F16)


def decoded(message, each):
    message = message.astype(F32)
    level = message[each : each + 1]
    return message * jnp.exp2(level), level


def in_order(later, earlier):
    return lax.optimization_barrier((later, earlier))


def partners(parts):
    return sorted(range(1, parts), key=lambda k: -bin(k).count("1"))


def sum_over_plane(keep, got, each, parts):
    level = jnp.maximum(keep[0, each : each + 1], got[0, each : each + 1]) + 1.0
    parts_got = {
        k: swapped_in_plane(coded(keep[k] + got[k], level, each), k) for k in partners(parts)
    }
    total = keep[0] + got[0]
    for k in partners(parts):
        values, its_level = decoded(parts_got[k], each)
        total = total + values
        level = jnp.maximum(level, its_level)
    return total, level + math.ceil(math.log2(parts))


def sum_over_lines(total, level, each):
    quads = lax.axis_size("sp") // 4
    message = coded(total, level, each)
    others = {k: swapped(message, 4 * k) for k in range(quads - 1, 0, -1)}
    terms = [decoded(message, each)] + [decoded(others[k], each) for k in range(1, quads)]
    while len(terms) > 1:
        terms = [
            (left[0] + right[0], jnp.maximum(left[1], right[1]) + 1.0)
            for left, right in zip(terms[::2], terms[1::2])
        ]
    return terms[0]


def spread_over_plane(total, level, each, parts):
    message = coded(total, level, each)
    slots = {k: swapped_in_plane(message, k) for k in partners(parts)}
    slots[0] = message
    return [slots[k] for k in range(parts)]


def call(body, outs, operands, scratch, flops, smem=0):
    vmem = pl.BlockSpec(memory_space=pltpu.VMEM)
    return pl.pallas_call(
        body,
        out_shape=outs,
        in_specs=[pl.BlockSpec(memory_space=pltpu.SMEM)] * smem + [vmem] * (len(operands) - smem),
        out_specs=jax.tree.map(lambda _: vmem, outs),
        scratch_shapes=scratch,
        compiler_params=pltpu.CompilerParams(vmem_limit_bytes=32 * 1024 * 1024),
        cost_estimate=pl.CostEstimate(flops=flops, bytes_accessed=4_000_000, transcendentals=0),
    )(*operands)


def per_device(volume, weight, cotangent):
    channels, z_cells, y_cells, x_cells = volume.shape
    slabs, pencils = lax.axis_size("sp"), lax.axis_size("gz")
    width = channels // GROUPS
    out_channels = weight.shape[4]
    out_z, out_y, out_x = cotangent.shape[1:]
    lines = z_cells * y_cells
    out_cells = slabs * pencils * out_z * out_y * out_x
    parts = 2 * pencils
    rows = 27 * width
    each = rows // 2 // parts
    padded = (each + 8) // 8 * 8
    at_z, at_y = lax.axis_index("sp"), lax.axis_index("gz")
    place = jnp.stack([at_z % 2, at_z // 2 % 2 * pencils + at_y]).astype(jnp.int32)
    shape = jax.ShapeDtypeStruct

    up_c = shifted(cotangent, -1, -1)
    up_y = shifted(cotangent, 0, -1)
    up_z = shifted(cotangent, -1, 0)
    planes, own = call(
        lay_out_body,
        (shape((lines, channels, x_cells), BF), shape((out_y, channels, x_cells), BF)),
        (volume, cotangent),
        [],
        500_000_000,
    )
    last = planes.reshape(z_cells, y_cells, channels, x_cells)

    share = shape((parts, padded, out_channels), F32)
    cots, keep, send = call(
        kernel_grad_body,
        (shape((2 * (out_y + 1), channels, x_cells), BF), share, share),
        (place, planes, own, up_z, up_y, up_c),
        [
            pltpu.VMEM((8, channels, out_y * out_x), BF),
            pltpu.VMEM((8, channels, out_y * out_x), BF),
            pltpu.VMEM((rows, out_channels), F32),
        ],
        500_000_000,
        smem=1,
    )
    plane, send = in_order(last[-1], send)
    from_z = shifted(plane, 1, 0)
    got = swapped(send, 1)
    weights = weight.reshape(27, width, out_channels)
    volume_grad = call(
        backward_body,
        shape(volume.shape, BF),
        (cots, weights),
        [
            pltpu.VMEM((27 * channels, out_channels), BF),
            pltpu.VMEM((8, channels, out_y * out_x), BF),
            pltpu.VMEM((lines, channels, x_cells), BF),
        ],
        1_000_000_000,
    )
    total, level = sum_over_plane(keep, got, each, parts)
    total, volume_grad = in_order(total, volume_grad)
    from_y = shifted(jnp.concatenate([from_z[-1:], last[:, -1]], axis=0), 0, 1)
    total, level = sum_over_lines(total, level, each)
    total, from_y = in_order(total, from_y)
    mine = spread_over_plane(total, level, each, parts)
    output = call(
        forward_body,
        shape(cotangent.shape, BF),
        (planes, from_z, from_y, weights),
        [
            pltpu.VMEM((27 * channels, out_channels), BF),
            pltpu.VMEM((27 * channels, out_y * out_x), BF),
        ],
        1_000_000_000,
    )
    mine, output = in_order(mine, output)
    other = swapped(jnp.stack(mine), 1)
    slots = [m.astype(F32) for m in mine] + [other[k].astype(F32) for k in range(parts)]
    kernel_grad = call(
        functools.partial(assemble_body, 1.0 / math.sqrt(out_cells), parts, each),
        shape((rows, out_channels), F32),
        (place, *slots),
        [pltpu.VMEM((2 * parts, each, out_channels), F32)],
        1_000_000,
        smem=1,
    ).reshape(weight.shape)
    return (output, volume_grad, kernel_grad)


def solution(mesh):
    in_specs = (P(None, "sp", "gz", None), P(), P(None, "sp", "gz", None))
    out_specs = (P(None, "sp", "gz", None), P(None, "sp", "gz", None), P())
    return jax.shard_map(
        per_device, mesh=mesh, in_specs=in_specs, out_specs=out_specs, check_vma=False
    )
```

```python
import functools
import math

import jax
import jax.numpy as jnp
from jax import lax
from jax.experimental import pallas as pl
from jax.experimental.pallas import tpu as pltpu
from jax.sharding import PartitionSpec as P

GROUPS = 2
BF = jnp.bfloat16
F32 = jnp.float32
F16 = jnp.float16


def dot(left, right, dims=((1,), (0,))):
    return lax.dot_general(left, right, (dims, ((), ())), preferred_element_type=F32)


def exact(left, right):
    return dot(left, right).astype(BF)


def ones_where(shape, condition):
    row = lax.broadcasted_iota(jnp.int32, shape, 0)
    col = lax.broadcasted_iota(jnp.int32, shape, 1)
    return jnp.where(condition(row, col), 1.0, 0.0).astype(BF)


def rows_grouped(block, inner):
    size = block * inner
    return ones_where((size, size), lambda row, col: col == (row % block) * inner + row // block)


def rows_interleaved(block, inner):
    size = block * inner
    return ones_where((size, size), lambda row, col: row == (col % block) * inner + col // block)


def taps_of(parity):
    return (1,) if parity == 0 else (0, 2)


def cotangent_rows(source_ref, count):
    channels, _, out_y, out_x = source_ref.shape
    by_row = rows_grouped(channels, out_y)
    return exact(by_row[: count * channels], source_ref[...].reshape(channels * out_y, out_x))


def kept(array, flag):
    return jnp.where(flag != 0, array, jnp.zeros_like(array))


def put_rows(rows, cots_ref, first):
    _, channels, x_cells = cots_ref.shape
    out_x = x_cells // 2
    both = exact(
        rows,
        ones_where(
            (out_x, x_cells),
            lambda row, col: row == jnp.where(col < out_x, col, col - out_x + 1),
        ),
    )
    for k in range(rows.shape[0] // channels):
        cots_ref[first + k] = both[k * channels : (k + 1) * channels]


def lay_out_body(vol_ref, own_ref, class_ref, cots_ref):
    channels, z_cells, y_cells, x_cells = vol_ref.shape
    out_x = x_cells // 2
    lines = z_cells * y_cells
    block = 256 // lines
    put_rows(cotangent_rows(own_ref, cots_ref.shape[0]), cots_ref, 0)
    by_line = rows_grouped(block, lines)
    halves = ones_where(
        (x_cells, x_cells),
        lambda row, col: row == jnp.where(col < out_x, 2 * col, 2 * (col - out_x) + 1),
    )
    for at in range(0, channels, block):
        rows = vol_ref[at : at + block].reshape(block * lines, x_cells)
        rows = exact(exact(by_line, rows), halves)
        for z in range(z_cells):
            for y in range(y_cells):
                k = z * y_cells + y
                line = rows[k * block : (k + 1) * block]
                for x_par in range(2):
                    class_ref[
                        (z * 2 + y % 2) * 2 + x_par,
                        at : at + block,
                        y // 2 * out_x : (y // 2 + 1) * out_x,
                    ] = line[:, x_par * out_x : (x_par + 1) * out_x]


def kernel_grad_body(
    place_ref, class_ref, own_ref, up_z_ref, up_y_ref, up_c_ref,
    cots_ref, keep_ref, send_ref, shift_ref, grad_ref,
):
    out_y, channels, _ = own_ref.shape
    width = channels // GROUPS

    cots_ref[:out_y] = own_ref[...]
    next_z, next_y = place_ref[3], place_ref[5]
    put_rows(kept(cotangent_rows(up_y_ref, 1), next_y), cots_ref, out_y)
    put_rows(kept(cotangent_rows(up_z_ref, out_y), next_z), cots_ref, out_y + 1)
    put_rows(kept(cotangent_rows(up_c_ref, 1), next_z * next_y), cots_ref, 2 * out_y + 1)
    pair_rows(cots_ref, shift_ref)

    first_half = lax.broadcasted_iota(jnp.int32, (width, channels), 1) < width
    for a in range(3):
        for b in range(3):
            for c in range(3):
                which = ((a != 1) * 2 + (b != 1)) * 2 + (c != 1)
                cot = ((a == 0) * 2 + (b == 0)) * 2 + (c == 0)
                full = dot(class_ref[which], shift_ref[cot], ((1,), (1,)))
                tap = (a * 3 + b) * 3 + c
                grad_ref[tap * width : (tap + 1) * width] = jnp.where(
                    first_half, full[:width], full[width:]
                )

    parts, padded, _ = keep_ref.shape
    half = grad_ref.shape[0] // 2
    each = half // parts
    top = jnp.maximum(jnp.max(jnp.abs(grad_ref[...])), 1e-30)
    level = jnp.floor(jnp.log2(jnp.full((padded - each, channels), top, F32))) - 14.0
    low = place_ref[0] == 0
    for part in range(parts):
        slot = place_ref[1] ^ part
        here = grad_ref[part * each : (part + 1) * each]
        there = grad_ref[half + part * each : half + (part + 1) * each]
        keep_ref[slot, :each] = jnp.where(low, here, there)
        send_ref[slot, :each] = jnp.where(low, there, here)
        keep_ref[slot, each:] = level
        send_ref[slot, each:] = level


def pair_rows(cots_ref, shift_ref):
    out_y = cots_ref.shape[0] // 2 - 1
    out_x = cots_ref.shape[2] // 2
    for plane in range(2):
        for off in range(2):
            for step in range(2):
                for y in range(out_y):
                    shift_ref[(plane * 2 + off) * 2 + step, :, y * out_x : (y + 1) * out_x] = cots_ref[
                        plane * (out_y + 1) + off + y, :, step * out_x : (step + 1) * out_x
                    ]


def spread_groups(weight_ref, spread_ref):
    _, width, channels = weight_ref.shape
    first_half = lax.broadcasted_iota(jnp.int32, (width, channels), 1) < width
    for tap in range(27):
        part = weight_ref[tap]
        zero = jnp.zeros_like(part)
        spread_ref[tap * channels : tap * channels + width] = jnp.where(first_half, part, zero)
        spread_ref[tap * channels + width : (tap + 1) * channels] = jnp.where(first_half, zero, part)


def forward_body(place_ref, class_ref, from_z_ref, from_y_ref, weight_ref, out_ref, spread_ref, patch_ref):
    _, channels, cells = class_ref.shape
    out_x = from_y_ref.shape[2]
    out_y = cells // out_x
    spread_groups(weight_ref, spread_ref)
    moved = ones_where((out_x, out_x), lambda row, col: row == col - 1)

    def piece(a, q, x_par):
        if q < 0:
            inside = place_ref[4] * place_ref[2] if a == 0 else place_ref[4]
            return kept(from_y_ref[a * 2 + x_par], inside)
        lanes = slice(q // 2 * out_x, (q // 2 + 1) * out_x)
        if a == 0:
            return kept(from_z_ref[q % 2 * 2 + x_par, :, lanes], place_ref[2])
        return class_ref[((a - 1) * 2 + q % 2) * 2 + x_par, :, lanes]

    for a in range(3):
        for q in range(-1, 2 * out_y):
            odd = piece(a, q, 1)
            pieces = (exact(odd, moved), piece(a, q, 0), odd)
            for b in taps_of(q % 2):
                y = (q + 1 - b) // 2
                if 0 <= y < out_y:
                    for c in range(3):
                        tap = (a * 3 + b) * 3 + c
                        patch_ref[
                            tap * channels : (tap + 1) * channels, y * out_x : (y + 1) * out_x
                        ] = pieces[c]
    result = dot(spread_ref[...], patch_ref[...], ((0,), (0,))).astype(BF)
    stacked = jnp.concatenate(
        [result[:, y * out_x : (y + 1) * out_x] for y in range(out_y)], axis=0
    )
    out_ref[...] = exact(rows_interleaved(channels, out_y), stacked).reshape(out_ref.shape)


def backward_body(cots_ref, weight_ref, grad_ref, spread_ref, shift_ref, lines_ref):
    channels, z_cells, y_cells, x_cells = grad_ref.shape
    lines = z_cells * y_cells
    out_x = x_cells // 2
    out_y = y_cells // 2
    spread_groups(weight_ref, spread_ref)
    pair_rows(cots_ref, shift_ref)

    for z in range(z_cells):
        for y_par in range(2):
            for x_par in range(2):
                total = jnp.zeros((channels, out_y * out_x), F32)
                for a in taps_of(z):
                    for b in taps_of(y_par):
                        for c in taps_of(x_par):
                            tap = (a * 3 + b) * 3 + c
                            cot = ((a == 0) * 2 + (b == 0)) * 2 + (c == 0)
                            total += dot(
                                spread_ref[tap * channels : (tap + 1) * channels], shift_ref[cot]
                            )
                total = total.astype(BF)
                for y in range(out_y):
                    lines_ref[
                        z * y_cells + 2 * y + y_par, :, x_par * out_x : (x_par + 1) * out_x
                    ] = total[:, y * out_x : (y + 1) * out_x]
    block = 256 // lines
    by_cell = rows_interleaved(block, lines)
    joined = ones_where(
        (x_cells, x_cells),
        lambda row, col: col == jnp.where(row < out_x, 2 * row, 2 * (row - out_x) + 1),
    )
    for at in range(0, channels, block):
        rows = jnp.concatenate([lines_ref[k, at : at + block, :] for k in range(lines)], axis=0)
        rows = exact(by_cell, exact(rows, joined))
        grad_ref[at : at + block] = rows.reshape(block, z_cells, y_cells, x_cells)


def assemble_body(scale, parts, each, place_ref, *refs):
    slots, out_ref, held_ref = refs[:-2], refs[-2], refs[-1]
    half = parts * each
    for k, slot_ref in enumerate(slots):
        held_ref[k] = slot_ref[:each] * (jnp.exp2(slot_ref[each : each + 1]) * scale)
    for side in range(2):
        for part in range(parts):
            slot = (place_ref[0] ^ side) * parts + (place_ref[1] ^ part)
            at = side * half + part * each
            out_ref[at : at + each] = held_ref[slot]


def shifted(array, by_z, by_y):
    size_z, size_y = lax.axis_size("sp"), lax.axis_size("gz")
    pairs = [
        (z * size_y + y, (z + by_z) % size_z * size_y + (y + by_y) % size_y)
        for z in range(size_z)
        for y in range(size_y)
    ]
    return lax.ppermute(array, ("sp", "gz"), pairs)


def swapped(array, flip):
    return lax.ppermute(array, "sp", [(i, i ^ flip) for i in range(lax.axis_size("sp"))])


def swapped_in_plane(array, flip):
    size_z, size_y = lax.axis_size("sp"), lax.axis_size("gz")
    pairs = []
    for z in range(size_z):
        for y in range(size_y):
            to = ((z // 2 % 2) * size_y + y) ^ flip
            to_z = z // 4 * 4 + to // size_y * 2 + z % 2
            pairs.append((z * size_y + y, to_z * size_y + to % size_y))
    return lax.ppermute(array, ("sp", "gz"), pairs)


def coded(values, level, each):
    row = lax.broadcasted_iota(jnp.int32, values.shape, values.ndim - 2)
    return jnp.where(row < each, values * jnp.exp2(-level), level).astype(F16)


def decoded(message, each):
    message = message.astype(F32)
    level = message[..., each : each + 1, :]
    return message * jnp.exp2(level), level


def in_order(*arrays):
    return lax.optimization_barrier(arrays)


def partners(parts):
    return sorted(range(1, parts), key=lambda k: -bin(k).count("1"))


def sum_over_plane(keep, got, each, parts):
    level = jnp.maximum(keep[0, each : each + 1], got[0, each : each + 1]) + 1.0
    parts_got = {
        k: swapped_in_plane(coded(keep[k] + got[k], level, each), k) for k in partners(parts)
    }
    total = keep[0] + got[0]
    for k in partners(parts):
        values, its_level = decoded(parts_got[k], each)
        total = total + values
        level = jnp.maximum(level, its_level)
    return total, level + math.ceil(math.log2(parts))


def sum_over_lines(total, level, each):
    quads = lax.axis_size("sp") // 4
    message = coded(total, level, each)
    others = {k: swapped(message, 4 * k) for k in range(quads - 1, 0, -1)}
    terms = [decoded(message, each)] + [decoded(others[k], each) for k in range(1, quads)]
    while len(terms) > 1:
        terms = [
            (left[0] + right[0], jnp.maximum(left[1], right[1]) + 1.0)
            for left, right in zip(terms[::2], terms[1::2])
        ]
    return terms[0]


def spread_over_plane(total, level, each, parts):
    message = coded(total, level, each)
    slots = {k: swapped_in_plane(message, k) for k in partners(parts)}
    slots[0] = message
    return [slots[k] for k in range(parts)]


def call(body, outs, operands, scratch=(), flops=1_000_000, spaces=None):
    vmem = pl.BlockSpec(memory_space=pltpu.VMEM)
    return pl.pallas_call(
        body,
        out_shape=outs,
        in_specs=[
            pl.BlockSpec(memory_space=(spaces or {}).get(k, pltpu.VMEM))
            for k in range(len(operands))
        ],
        out_specs=jax.tree.map(lambda _: vmem, outs),
        scratch_shapes=scratch,
        compiler_params=pltpu.CompilerParams(vmem_limit_bytes=32 * 1024 * 1024),
        cost_estimate=pl.CostEstimate(flops=flops, bytes_accessed=4_000_000, transcendentals=0),
    )(*operands)


def per_device(volume, weight, cotangent):
    channels, z_cells, y_cells, x_cells = volume.shape
    slabs, pencils = lax.axis_size("sp"), lax.axis_size("gz")
    width = channels // GROUPS
    out_channels = weight.shape[4]
    out_z, out_y, out_x = cotangent.shape[1:]
    lines = z_cells * y_cells
    cells = out_y * out_x
    out_cells = slabs * pencils * out_z * out_y * out_x
    parts = 2 * pencils
    rows = 27 * width
    each = rows // 2 // parts
    padded = (each + 8) // 8 * 8
    at_z, at_y = lax.axis_index("sp"), lax.axis_index("gz")
    place = jnp.stack(
        [
            at_z % 2,
            at_z // 2 % 2 * pencils + at_y,
            (at_z > 0) * 1,
            (at_z < slabs - 1) * 1,
            (at_y > 0) * 1,
            (at_y < pencils - 1) * 1,
        ]
    ).astype(jnp.int32)
    shape = jax.ShapeDtypeStruct

    up_z = shifted(cotangent, -1, 0)
    up_c = shifted(cotangent, -1, -1)
    up_y = shifted(cotangent, 0, -1)
    classes, own = call(
        lay_out_body,
        (shape((8, channels, cells), BF), shape((out_y, channels, x_cells), BF)),
        (volume, cotangent),
        [],
        500_000_000,
    )
    share = shape((parts, padded, out_channels), F32)
    cots, keep, send = call(
        kernel_grad_body,
        (shape((2 * (out_y + 1), channels, x_cells), BF), share, share),
        (place, classes, own, up_z, up_y, up_c),
        [pltpu.VMEM((8, channels, cells), BF), pltpu.VMEM((rows, out_channels), F32)],
        500000000,
        {0: pltpu.SMEM},
    )
    plane, send = in_order(classes[4:], send)
    from_z = shifted(plane, 1, 0)
    got = swapped(send, 1)
    weights = weight.reshape(27, width, out_channels)
    spread = pltpu.VMEM((27 * channels, out_channels), BF)
    volume_grad = call(
        backward_body,
        shape(volume.shape, BF),
        (cots, weights),
        [
            spread,
            pltpu.VMEM((8, channels, cells), BF),
            pltpu.VMEM((lines, channels, x_cells), BF),
        ],
        1_000_000_000,
    )
    total, level = sum_over_plane(keep, got, each, parts)
    total, volume_grad = in_order(total, volume_grad)
    total, from_z = in_order(total, from_z)
    edge = jnp.concatenate([from_z[2:], classes[2:4], classes[6:]], axis=0)[:, :, cells - out_x :]
    from_y = shifted(edge, 0, 1)
    total, level = sum_over_lines(total, level, each)
    total, from_y = in_order(total, from_y)
    mine = spread_over_plane(total, level, each, parts)
    output = call(
        forward_body,
        shape(cotangent.shape, BF),
        (place, classes, from_z, from_y, weights),
        [spread, pltpu.VMEM((27 * channels, cells), BF)],
        1_000_000_000,
        {0: pltpu.SMEM},
    )
    mine, output = in_order(mine, output)
    other = swapped(jnp.stack(mine), 1)
    slots = [m.astype(F32) for m in mine] + [other[k].astype(F32) for k in range(parts)]
    kernel_grad = call(
        functools.partial(assemble_body, 1.0 / math.sqrt(out_cells), parts, each),
        shape((rows, out_channels), F32),
        (place, *slots),
        [pltpu.VMEM((2 * parts, each, out_channels), F32)],
        1_000_000,
        {0: pltpu.SMEM},
    ).reshape(weight.shape)
    return (output, volume_grad, kernel_grad)


def solution(mesh):
    in_specs = (P(None, "sp", "gz", None), P(), P(None, "sp", "gz", None))
    out_specs = (P(None, "sp", "gz", None), P(None, "sp", "gz", None), P())
    return jax.shard_map(
        per_device, mesh=mesh, in_specs=in_specs, out_specs=out_specs, check_vma=False
    )
```

```python
import functools
import math

import jax
import jax.numpy as jnp
from jax import lax
from jax.experimental import pallas as pl
from jax.experimental.pallas import tpu as pltpu
from jax.sharding import PartitionSpec as P

GROUPS = 2
BF = jnp.bfloat16
F32 = jnp.float32
F16 = jnp.float16


def dot(left, right, dims=((1,), (0,))):
    return lax.dot_general(left, right, (dims, ((), ())), preferred_element_type=F32)


def exact(left, right):
    return dot(left, right).astype(BF)


def ones_where(shape, condition):
    row = lax.broadcasted_iota(jnp.int32, shape, 0)
    col = lax.broadcasted_iota(jnp.int32, shape, 1)
    return jnp.where(condition(row, col), 1.0, 0.0).astype(BF)


def rows_grouped(block, inner):
    size = block * inner
    return ones_where((size, size), lambda row, col: col == (row % block) * inner + row // block)


def rows_interleaved(block, inner):
    size = block * inner
    return ones_where((size, size), lambda row, col: row == (col % block) * inner + col // block)


def taps_of(parity):
    return (1,) if parity == 0 else (0, 2)


def cotangent_rows(source_ref, count):
    channels, _, out_y, out_x = source_ref.shape
    by_row = rows_grouped(channels, out_y)
    return exact(by_row[: count * channels], source_ref[...].reshape(channels * out_y, out_x))


def place():
    at_z, at_y = lax.axis_index("sp"), lax.axis_index("gz")
    return at_z % 2, at_z // 2 % 2 * lax.axis_size("gz") + at_y


def kept(array, flag):
    return jnp.where(flag != 0, array, jnp.zeros_like(array))


def put_rows(rows, cots_ref, first):
    _, channels, x_cells = cots_ref.shape
    out_x = x_cells // 2
    both = exact(
        rows,
        ones_where(
            (out_x, x_cells),
            lambda row, col: row == jnp.where(col < out_x, col, col - out_x + 1),
        ),
    )
    for k in range(rows.shape[0] // channels):
        cots_ref[first + k] = both[k * channels : (k + 1) * channels]


def lay_out_body(vol_ref, own_ref, class_ref, cots_ref):
    channels, z_cells, y_cells, x_cells = vol_ref.shape
    out_x = x_cells // 2
    lines = z_cells * y_cells
    block = 256 // lines
    put_rows(cotangent_rows(own_ref, cots_ref.shape[0]), cots_ref, 0)
    by_line = rows_grouped(block, lines)
    halves = ones_where(
        (x_cells, x_cells),
        lambda row, col: row == jnp.where(col < out_x, 2 * col, 2 * (col - out_x) + 1),
    )
    for at in range(0, channels, block):
        rows = vol_ref[at : at + block].reshape(block * lines, x_cells)
        rows = exact(exact(by_line, rows), halves)
        for z in range(z_cells):
            for y in range(y_cells):
                k = z * y_cells + y
                line = rows[k * block : (k + 1) * block]
                for x_par in range(2):
                    class_ref[
                        (z * 2 + y % 2) * 2 + x_par,
                        at : at + block,
                        y // 2 * out_x : (y // 2 + 1) * out_x,
                    ] = line[:, x_par * out_x : (x_par + 1) * out_x]


def kernel_grad_body(
    class_ref, own_ref, up_z_ref, up_y_ref, up_c_ref,
    cots_ref, keep_ref, send_ref, shift_ref, grad_ref,
):
    out_y, channels, _ = own_ref.shape
    width = channels // GROUPS

    cots_ref[:out_y] = own_ref[...]
    next_z = (lax.axis_index("sp") < lax.axis_size("sp") - 1) * 1
    next_y = (lax.axis_index("gz") < lax.axis_size("gz") - 1) * 1
    put_rows(kept(cotangent_rows(up_y_ref, 1), next_y), cots_ref, out_y)
    put_rows(kept(cotangent_rows(up_z_ref, out_y), next_z), cots_ref, out_y + 1)
    put_rows(kept(cotangent_rows(up_c_ref, 1), next_z * next_y), cots_ref, 2 * out_y + 1)
    pair_rows(cots_ref, shift_ref)

    first_half = lax.broadcasted_iota(jnp.int32, (width, channels), 1) < width
    for a in range(3):
        for b in range(3):
            for c in range(3):
                which = ((a != 1) * 2 + (b != 1)) * 2 + (c != 1)
                cot = ((a == 0) * 2 + (b == 0)) * 2 + (c == 0)
                full = dot(class_ref[which], shift_ref[cot], ((1,), (1,)))
                tap = (a * 3 + b) * 3 + c
                grad_ref[tap * width : (tap + 1) * width] = jnp.where(
                    first_half, full[:width], full[width:]
                )

    parts, padded, _ = keep_ref.shape
    half = grad_ref.shape[0] // 2
    each = half // parts
    top = jnp.maximum(jnp.max(jnp.abs(grad_ref[...])), 1e-30)
    level = jnp.floor(jnp.log2(jnp.full((padded - each, channels), top, F32))) - 14.0
    core, at = place()
    low = core == 0
    for part in range(parts):
        slot = at ^ part
        here = grad_ref[part * each : (part + 1) * each]
        there = grad_ref[half + part * each : half + (part + 1) * each]
        keep_ref[slot, :each] = jnp.where(low, here, there)
        send_ref[slot, :each] = jnp.where(low, there, here)
        keep_ref[slot, each:] = level
        send_ref[slot, each:] = level


def pair_rows(cots_ref, shift_ref):
    out_y = cots_ref.shape[0] // 2 - 1
    out_x = cots_ref.shape[2] // 2
    for plane in range(2):
        for off in range(2):
            for step in range(2):
                for y in range(out_y):
                    shift_ref[(plane * 2 + off) * 2 + step, :, y * out_x : (y + 1) * out_x] = cots_ref[
                        plane * (out_y + 1) + off + y, :, step * out_x : (step + 1) * out_x
                    ]


def spread_groups(weight_ref, spread_ref):
    _, width, channels = weight_ref.shape
    first_half = lax.broadcasted_iota(jnp.int32, (width, channels), 1) < width
    for tap in range(27):
        part = weight_ref[tap]
        zero = jnp.zeros_like(part)
        spread_ref[tap * channels : tap * channels + width] = jnp.where(first_half, part, zero)
        spread_ref[tap * channels + width : (tap + 1) * channels] = jnp.where(first_half, zero, part)


def forward_body(class_ref, from_z_ref, from_y_ref, weight_ref, out_ref, spread_ref, patch_ref):
    _, channels, cells = class_ref.shape
    out_x = from_y_ref.shape[2]
    out_y = cells // out_x
    spread_groups(weight_ref, spread_ref)
    moved = ones_where((out_x, out_x), lambda row, col: row == col - 1)

    def piece(a, q, x_par):
        if q < 0:
            return from_y_ref[a * 2 + x_par]
        lanes = slice(q // 2 * out_x, (q // 2 + 1) * out_x)
        if a == 0:
            return from_z_ref[q % 2 * 2 + x_par, :, lanes]
        return class_ref[((a - 1) * 2 + q % 2) * 2 + x_par, :, lanes]

    for a in range(3):
        for q in range(-1, 2 * out_y):
            odd = piece(a, q, 1)
            pieces = (exact(odd, moved), piece(a, q, 0), odd)
            for b in taps_of(q % 2):
                y = (q + 1 - b) // 2
                if 0 <= y < out_y:
                    for c in range(3):
                        tap = (a * 3 + b) * 3 + c
                        patch_ref[
                            tap * channels : (tap + 1) * channels, y * out_x : (y + 1) * out_x
                        ] = pieces[c]

    @pl.when(lax.axis_index("sp") == 0)
    def _():
        patch_ref[: 9 * channels] = jnp.zeros_like(patch_ref[: 9 * channels])

    @pl.when(lax.axis_index("gz") == 0)
    def _():
        for a in range(3):
            at = a * 9 * channels
            first = patch_ref.at[at : at + 3 * channels, :out_x]
            first[...] = jnp.zeros_like(first)

    result = dot(spread_ref[...], patch_ref[...], ((0,), (0,))).astype(BF)
    stacked = jnp.concatenate(
        [result[:, y * out_x : (y + 1) * out_x] for y in range(out_y)], axis=0
    )
    out_ref[...] = exact(rows_interleaved(channels, out_y), stacked).reshape(out_ref.shape)


def backward_body(cots_ref, weight_ref, grad_ref, spread_ref, shift_ref, lines_ref):
    channels, z_cells, y_cells, x_cells = grad_ref.shape
    lines = z_cells * y_cells
    out_x = x_cells // 2
    out_y = y_cells // 2
    spread_groups(weight_ref, spread_ref)
    pair_rows(cots_ref, shift_ref)

    for z in range(z_cells):
        for y_par in range(2):
            for x_par in range(2):
                total = jnp.zeros((channels, out_y * out_x), F32)
                for a in taps_of(z):
                    for b in taps_of(y_par):
                        for c in taps_of(x_par):
                            tap = (a * 3 + b) * 3 + c
                            cot = ((a == 0) * 2 + (b == 0)) * 2 + (c == 0)
                            total += dot(
                                spread_ref[tap * channels : (tap + 1) * channels], shift_ref[cot]
                            )
                total = total.astype(BF)
                for y in range(out_y):
                    lines_ref[
                        z * y_cells + 2 * y + y_par, :, x_par * out_x : (x_par + 1) * out_x
                    ] = total[:, y * out_x : (y + 1) * out_x]
    block = 256 // lines
    by_cell = rows_interleaved(block, lines)
    joined = ones_where(
        (x_cells, x_cells),
        lambda row, col: col == jnp.where(row < out_x, 2 * row, 2 * (row - out_x) + 1),
    )
    for at in range(0, channels, block):
        rows = jnp.concatenate([lines_ref[k, at : at + block, :] for k in range(lines)], axis=0)
        rows = exact(by_cell, exact(rows, joined))
        grad_ref[at : at + block] = rows.reshape(block, z_cells, y_cells, x_cells)


def assemble_body(scale, parts, each, *refs):
    slots, out_ref, held_ref = refs[:-2], refs[-2], refs[-1]
    half = parts * each
    for k, slot_ref in enumerate(slots):
        held_ref[k] = slot_ref[:each] * (jnp.exp2(slot_ref[each : each + 1]) * scale)
    core, mine = place()
    for side in range(2):
        for part in range(parts):
            slot = (core ^ side) * parts + (mine ^ part)
            at = side * half + part * each
            out_ref[at : at + each] = held_ref[slot]


def shifted(array, by_z, by_y):
    size_z, size_y = lax.axis_size("sp"), lax.axis_size("gz")
    pairs = [
        (z * size_y + y, (z + by_z) % size_z * size_y + (y + by_y) % size_y)
        for z in range(size_z)
        for y in range(size_y)
    ]
    return lax.ppermute(array, ("sp", "gz"), pairs)


def swapped(array, flip):
    return lax.ppermute(array, "sp", [(i, i ^ flip) for i in range(lax.axis_size("sp"))])


def swapped_in_plane(array, flip):
    size_z, size_y = lax.axis_size("sp"), lax.axis_size("gz")
    pairs = []
    for z in range(size_z):
        for y in range(size_y):
            to = ((z // 2 % 2) * size_y + y) ^ flip
            to_z = z // 4 * 4 + to // size_y * 2 + z % 2
            pairs.append((z * size_y + y, to_z * size_y + to % size_y))
    return lax.ppermute(array, ("sp", "gz"), pairs)


def coded(values, level, each):
    row = lax.broadcasted_iota(jnp.int32, values.shape, values.ndim - 2)
    return jnp.where(row < each, values * jnp.exp2(-level), level).astype(F16)


def decoded(message, each):
    message = message.astype(F32)
    level = message[..., each : each + 1, :]
    return message * jnp.exp2(level), level


def in_order(*arrays):
    return lax.optimization_barrier(arrays)


def partners(parts):
    return sorted(range(1, parts), key=lambda k: -bin(k).count("1"))


def sum_over_plane(keep, got, each, parts):
    level = jnp.maximum(keep[0, each : each + 1], got[0, each : each + 1]) + 1.0
    parts_got = {
        k: swapped_in_plane(coded(keep[k] + got[k], level, each), k) for k in partners(parts)
    }
    total = keep[0] + got[0]
    for k in partners(parts):
        values, its_level = decoded(parts_got[k], each)
        total = total + values
        level = jnp.maximum(level, its_level)
    return total, level + math.ceil(math.log2(parts))


def sum_over_lines(total, level, each):
    quads = lax.axis_size("sp") // 4
    message = coded(total, level, each)
    others = {k: swapped(message, 4 * k) for k in range(quads - 1, 0, -1)}
    terms = [decoded(message, each)] + [decoded(others[k], each) for k in range(1, quads)]
    while len(terms) > 1:
        terms = [
            (left[0] + right[0], jnp.maximum(left[1], right[1]) + 1.0)
            for left, right in zip(terms[::2], terms[1::2])
        ]
    return terms[0]


def spread_over_plane(total, level, each, parts):
    message = coded(total, level, each)
    slots = {k: swapped_in_plane(message, k) for k in partners(parts)}
    slots[0] = message
    return [slots[k] for k in range(parts)]


def call(body, outs, operands, scratch=(), flops=1_000_000, spaces=None):
    vmem = pl.BlockSpec(memory_space=pltpu.VMEM)
    return pl.pallas_call(
        body,
        out_shape=outs,
        in_specs=[
            pl.BlockSpec(memory_space=(spaces or {}).get(k, pltpu.VMEM))
            for k in range(len(operands))
        ],
        out_specs=jax.tree.map(lambda _: vmem, outs),
        scratch_shapes=scratch,
        compiler_params=pltpu.CompilerParams(vmem_limit_bytes=32 * 1024 * 1024),
        cost_estimate=pl.CostEstimate(flops=flops, bytes_accessed=4_000_000, transcendentals=0),
    )(*operands)


def per_device(volume, weight, cotangent):
    channels, z_cells, y_cells, x_cells = volume.shape
    slabs, pencils = lax.axis_size("sp"), lax.axis_size("gz")
    width = channels // GROUPS
    out_channels = weight.shape[4]
    out_z, out_y, out_x = cotangent.shape[1:]
    lines = z_cells * y_cells
    cells = out_y * out_x
    out_cells = slabs * pencils * out_z * out_y * out_x
    parts = 2 * pencils
    rows = 27 * width
    each = rows // 2 // parts
    padded = (each + 8) // 8 * 8
    shape = jax.ShapeDtypeStruct

    up_z = shifted(cotangent, -1, 0)
    up_c = shifted(cotangent, -1, -1)
    up_y = shifted(cotangent, 0, -1)
    classes, own = call(
        lay_out_body,
        (shape((8, channels, cells), BF), shape((out_y, channels, x_cells), BF)),
        (volume, cotangent),
        [],
        0,
    )
    share = shape((parts, padded, out_channels), F32)
    cots, keep, send = call(
        kernel_grad_body,
        (shape((2 * (out_y + 1), channels, x_cells), BF), share, share),
        (classes, own, up_z, up_y, up_c),
        [pltpu.VMEM((8, channels, cells), BF), pltpu.VMEM((rows, out_channels), F32)],
        500000000,
    )
    plane, send = in_order(classes[4:], send)
    from_z = shifted(plane, 1, 0)
    got = swapped(send, 1)
    weights = weight.reshape(27, width, out_channels)
    spread = pltpu.VMEM((27 * channels, out_channels), BF)
    volume_grad = call(
        backward_body,
        shape(volume.shape, BF),
        (cots, weights),
        [
            spread,
            pltpu.VMEM((8, channels, cells), BF),
            pltpu.VMEM((lines, channels, x_cells), BF),
        ],
        1_000_000_000,
    )
    total, level = sum_over_plane(keep, got, each, parts)
    total, volume_grad = in_order(total, volume_grad)
    total, from_z = in_order(total, from_z)
    edge = jnp.concatenate([from_z[2:], classes[2:4], classes[6:]], axis=0)[:, :, cells - out_x :]
    from_y = shifted(edge, 0, 1)
    total, level = sum_over_lines(total, level, each)
    mine = spread_over_plane(total, level, each, parts)
    output = call(
        forward_body,
        shape(cotangent.shape, BF),
        (classes, from_z, from_y, weights),
        [spread, pltpu.VMEM((27 * channels, cells), BF)],
        1_000_000_000,
    )
    mine, output = in_order(mine, output)
    other = swapped(jnp.stack(mine), 1)
    slots = [m.astype(F32) for m in mine] + [other[k].astype(F32) for k in range(parts)]
    kernel_grad = call(
        functools.partial(assemble_body, 1.0 / math.sqrt(out_cells), parts, each),
        shape((rows, out_channels), F32),
        tuple(slots),
        [pltpu.VMEM((2 * parts, each, out_channels), F32)],
        1_000_000,
    ).reshape(weight.shape)
    return (output, volume_grad, kernel_grad)


def solution(mesh):
    in_specs = (P(None, "sp", "gz", None), P(), P(None, "sp", "gz", None))
    out_specs = (P(None, "sp", "gz", None), P(None, "sp", "gz", None), P())
    return jax.shard_map(
        per_device, mesh=mesh, in_specs=in_specs, out_specs=out_specs, check_vma=False
    )
```

```python
import functools
import math

import jax
import jax.numpy as jnp
from jax import lax
from jax.experimental import pallas as pl
from jax.experimental.pallas import tpu as pltpu
from jax.sharding import PartitionSpec as P

GROUPS = 2
BF = jnp.bfloat16
F32 = jnp.float32
F16 = jnp.float16


def dot(left, right, dims=((1,), (0,))):
    return lax.dot_general(left, right, (dims, ((), ())), preferred_element_type=F32)


def exact(left, right):
    return dot(left, right).astype(BF)


def ones_where(shape, condition):
    row = lax.broadcasted_iota(jnp.int32, shape, 0)
    col = lax.broadcasted_iota(jnp.int32, shape, 1)
    return jnp.where(condition(row, col), 1.0, 0.0).astype(BF)


def rows_grouped(block, inner):
    size = block * inner
    return ones_where((size, size), lambda row, col: col == (row % block) * inner + row // block)


def rows_interleaved(block, inner):
    size = block * inner
    return ones_where((size, size), lambda row, col: row == (col % block) * inner + col // block)


def taps_of(parity):
    return (1,) if parity == 0 else (0, 2)


def cotangent_rows(source_ref, count):
    channels, _, out_y, out_x = source_ref.shape
    by_row = rows_grouped(channels, out_y)
    return exact(by_row[: count * channels], source_ref[...].reshape(channels * out_y, out_x))


def place():
    at_z, at_y = lax.axis_index("sp"), lax.axis_index("gz")
    return at_z % 2, at_z // 2 % 2 * lax.axis_size("gz") + at_y


def kept(array, flag):
    return jnp.where(flag != 0, array, jnp.zeros_like(array))


def put_rows(rows, cots_ref, first):
    _, channels, x_cells = cots_ref.shape
    out_x = x_cells // 2
    both = exact(
        rows,
        ones_where(
            (out_x, x_cells),
            lambda row, col: row == jnp.where(col < out_x, col, col - out_x + 1),
        ),
    )
    for k in range(rows.shape[0] // channels):
        cots_ref[first + k] = both[k * channels : (k + 1) * channels]


def lay_out_body(vol_ref, own_ref, class_ref, cots_ref):
    channels, z_cells, y_cells, x_cells = vol_ref.shape
    out_x = x_cells // 2
    lines = z_cells * y_cells
    block = 256 // lines
    put_rows(cotangent_rows(own_ref, cots_ref.shape[0]), cots_ref, 0)
    by_line = rows_grouped(block, lines)
    halves = ones_where(
        (x_cells, x_cells),
        lambda row, col: row == jnp.where(col < out_x, 2 * col, 2 * (col - out_x) + 1),
    )
    for at in range(0, channels, block):
        rows = vol_ref[at : at + block].reshape(block * lines, x_cells)
        rows = exact(exact(by_line, rows), halves)
        for z in range(z_cells):
            for y in range(y_cells):
                k = z * y_cells + y
                line = rows[k * block : (k + 1) * block]
                for x_par in range(2):
                    class_ref[
                        (z * 2 + y % 2) * 2 + x_par,
                        at : at + block,
                        y // 2 * out_x : (y // 2 + 1) * out_x,
                    ] = line[:, x_par * out_x : (x_par + 1) * out_x]


def kernel_grad_body(
    class_ref, own_ref, up_z_ref, up_y_ref, up_c_ref,
    cots_ref, keep_ref, send_ref, shift_ref, grad_ref,
):
    out_y, channels, _ = own_ref.shape
    width = channels // GROUPS

    cots_ref[:out_y] = own_ref[...]
    next_z = (lax.axis_index("sp") < lax.axis_size("sp") - 1) * 1
    next_y = (lax.axis_index("gz") < lax.axis_size("gz") - 1) * 1
    put_rows(kept(cotangent_rows(up_y_ref, 1), next_y), cots_ref, out_y)
    put_rows(kept(cotangent_rows(up_z_ref, out_y), next_z), cots_ref, out_y + 1)
    put_rows(kept(cotangent_rows(up_c_ref, 1), next_z * next_y), cots_ref, 2 * out_y + 1)
    pair_rows(cots_ref, shift_ref)

    first_half = lax.broadcasted_iota(jnp.int32, (width, channels), 1) < width
    for a in range(3):
        for b in range(3):
            for c in range(3):
                which = ((a != 1) * 2 + (b != 1)) * 2 + (c != 1)
                cot = ((a == 0) * 2 + (b == 0)) * 2 + (c == 0)
                full = dot(class_ref[which], shift_ref[cot], ((1,), (1,)))
                tap = (a * 3 + b) * 3 + c
                grad_ref[tap * width : (tap + 1) * width] = jnp.where(
                    first_half, full[:width], full[width:]
                )

    parts, padded, _ = keep_ref.shape
    half = grad_ref.shape[0] // 2
    each = half // parts
    top = jnp.maximum(jnp.max(jnp.abs(grad_ref[...])), 1e-30)
    level = jnp.floor(jnp.log2(jnp.full((padded - each, channels), top, F32))) - 14.0
    core, at = place()
    low = core == 0
    for part in range(parts):
        slot = at ^ part
        here = grad_ref[part * each : (part + 1) * each]
        there = grad_ref[half + part * each : half + (part + 1) * each]
        keep_ref[slot, :each] = jnp.where(low, here, there)
        send_ref[slot, :each] = jnp.where(low, there, here)
        keep_ref[slot, each:] = level
        send_ref[slot, each:] = level


def pair_rows(cots_ref, shift_ref):
    out_y = cots_ref.shape[0] // 2 - 1
    out_x = cots_ref.shape[2] // 2
    for plane in range(2):
        for off in range(2):
            for step in range(2):
                for y in range(out_y):
                    shift_ref[(plane * 2 + off) * 2 + step, :, y * out_x : (y + 1) * out_x] = cots_ref[
                        plane * (out_y + 1) + off + y, :, step * out_x : (step + 1) * out_x
                    ]


def spread_groups(weight_ref, spread_ref):
    _, width, channels = weight_ref.shape
    first_half = lax.broadcasted_iota(jnp.int32, (width, channels), 1) < width
    for tap in range(27):
        part = weight_ref[tap]
        zero = jnp.zeros_like(part)
        spread_ref[tap * channels : tap * channels + width] = jnp.where(first_half, part, zero)
        spread_ref[tap * channels + width : (tap + 1) * channels] = jnp.where(first_half, zero, part)


def forward_body(class_ref, from_z_ref, from_y_ref, weight_ref, out_ref, spread_ref, patch_ref):
    _, channels, cells = class_ref.shape
    out_x = from_y_ref.shape[2]
    out_y = cells // out_x
    spread_groups(weight_ref, spread_ref)
    moved = ones_where((out_x, out_x), lambda row, col: row == col - 1)

    def piece(a, q, x_par):
        if q < 0:
            return from_y_ref[a * 2 + x_par]
        lanes = slice(q // 2 * out_x, (q // 2 + 1) * out_x)
        if a == 0:
            return from_z_ref[q % 2 * 2 + x_par, :, lanes]
        return class_ref[((a - 1) * 2 + q % 2) * 2 + x_par, :, lanes]

    for a in range(3):
        for q in range(-1, 2 * out_y):
            odd = piece(a, q, 1)
            pieces = (exact(odd, moved), piece(a, q, 0), odd)
            for b in taps_of(q % 2):
                y = (q + 1 - b) // 2
                if 0 <= y < out_y:
                    for c in range(3):
                        tap = (a * 3 + b) * 3 + c
                        patch_ref[
                            tap * channels : (tap + 1) * channels, y * out_x : (y + 1) * out_x
                        ] = pieces[c]

    @pl.when(lax.axis_index("sp") == 0)
    def _():
        patch_ref[: 9 * channels] = jnp.zeros_like(patch_ref[: 9 * channels])

    @pl.when(lax.axis_index("gz") == 0)
    def _():
        for a in range(3):
            at = a * 9 * channels
            first = patch_ref.at[at : at + 3 * channels, :out_x]
            first[...] = jnp.zeros_like(first)

    result = dot(spread_ref[...], patch_ref[...], ((0,), (0,))).astype(BF)
    stacked = jnp.concatenate(
        [result[:, y * out_x : (y + 1) * out_x] for y in range(out_y)], axis=0
    )
    out_ref[...] = exact(rows_interleaved(channels, out_y), stacked).reshape(out_ref.shape)


def backward_body(cots_ref, weight_ref, grad_ref, spread_ref, shift_ref, lines_ref):
    channels, z_cells, y_cells, x_cells = grad_ref.shape
    lines = z_cells * y_cells
    out_x = x_cells // 2
    out_y = y_cells // 2
    spread_groups(weight_ref, spread_ref)
    pair_rows(cots_ref, shift_ref)

    for z in range(z_cells):
        for y_par in range(2):
            for x_par in range(2):
                total = jnp.zeros((channels, out_y * out_x), F32)
                for a in taps_of(z):
                    for b in taps_of(y_par):
                        for c in taps_of(x_par):
                            tap = (a * 3 + b) * 3 + c
                            cot = ((a == 0) * 2 + (b == 0)) * 2 + (c == 0)
                            total += dot(
                                spread_ref[tap * channels : (tap + 1) * channels], shift_ref[cot]
                            )
                total = total.astype(BF)
                for y in range(out_y):
                    lines_ref[
                        z * y_cells + 2 * y + y_par, :, x_par * out_x : (x_par + 1) * out_x
                    ] = total[:, y * out_x : (y + 1) * out_x]
    block = 256 // lines
    by_cell = rows_interleaved(block, lines)
    joined = ones_where(
        (x_cells, x_cells),
        lambda row, col: col == jnp.where(row < out_x, 2 * row, 2 * (row - out_x) + 1),
    )
    for at in range(0, channels, block):
        rows = jnp.concatenate([lines_ref[k, at : at + block, :] for k in range(lines)], axis=0)
        rows = exact(by_cell, exact(rows, joined))
        grad_ref[at : at + block] = rows.reshape(block, z_cells, y_cells, x_cells)


def assemble_body(scale, side, parts, each, *refs):
    slots, (out_ref, held_ref, half_ref, done) = refs[:parts], refs[-4:]
    core, mine = place()
    for k, slot_ref in enumerate(slots):
        held_ref[k] = slot_ref[:each] * (jnp.exp2(slot_ref[each : each + 1]) * scale)
    rows = parts * each
    start = (core ^ side) * rows
    split = parts if each % 8 == 0 else 1
    copies = []
    for at in range(0, rows, rows // split):
        for part in range(at // each, (at + rows // split) // each):
            half_ref[part * each : (part + 1) * each] = held_ref[mine ^ part]
        copies.append(
            pltpu.make_async_copy(
                half_ref.at[pl.ds(at, rows // split)],
                out_ref.at[pl.ds(pl.multiple_of(start + at, 8), rows // split)],
                done.at[len(copies)],
            )
        )
        copies[-1].start()
    for copy in copies:
        copy.wait()


def shifted(array, by_z, by_y):
    size_z, size_y = lax.axis_size("sp"), lax.axis_size("gz")
    pairs = [
        (z * size_y + y, (z + by_z) % size_z * size_y + (y + by_y) % size_y)
        for z in range(size_z)
        for y in range(size_y)
    ]
    return lax.ppermute(array, ("sp", "gz"), pairs)


def swapped(array, flip):
    return lax.ppermute(array, "sp", [(i, i ^ flip) for i in range(lax.axis_size("sp"))])


def swapped_in_plane(array, flip):
    size_z, size_y = lax.axis_size("sp"), lax.axis_size("gz")
    pairs = []
    for z in range(size_z):
        for y in range(size_y):
            to = ((z // 2 % 2) * size_y + y) ^ flip
            to_z = z // 4 * 4 + to // size_y * 2 + z % 2
            pairs.append((z * size_y + y, to_z * size_y + to % size_y))
    return lax.ppermute(array, ("sp", "gz"), pairs)


def coded(values, level, each):
    row = lax.broadcasted_iota(jnp.int32, values.shape, values.ndim - 2)
    return jnp.where(row < each, values * jnp.exp2(-level), level).astype(F16)


def decoded(message, each):
    message = message.astype(F32)
    level = message[..., each : each + 1, :]
    return message * jnp.exp2(level), level


def in_order(*arrays):
    return lax.optimization_barrier(arrays)


def partners(parts):
    return sorted(range(1, parts), key=lambda k: -bin(k).count("1"))


def sum_over_plane(keep, got, each, parts):
    level = jnp.maximum(keep[0, each : each + 1], got[0, each : each + 1]) + 1.0
    parts_got = {
        k: swapped_in_plane(coded(keep[k] + got[k], level, each), k) for k in partners(parts)
    }
    total = keep[0] + got[0]
    for k in partners(parts):
        values, its_level = decoded(parts_got[k], each)
        total = total + values
        level = jnp.maximum(level, its_level)
    return total, level + math.ceil(math.log2(parts))


def sum_over_lines(total, level, each):
    quads = lax.axis_size("sp") // 4
    message = coded(total, level, each)
    others = {k: swapped(message, 4 * k) for k in range(quads - 1, 0, -1)}
    terms = [decoded(message, each)] + [decoded(others[k], each) for k in range(1, quads)]
    while len(terms) > 1:
        terms = [
            (left[0] + right[0], jnp.maximum(left[1], right[1]) + 1.0)
            for left, right in zip(terms[::2], terms[1::2])
        ]
    return terms[0]


def spread_over_plane(total, level, each, parts):
    message = coded(total, level, each)
    slots = {k: swapped_in_plane(message, k) for k in partners(parts)}
    slots[0] = message
    return [slots[k] for k in range(parts)]


def call(body, outs, operands, scratch=(), flops=1_000_000, spaces=None):
    vmem = pl.BlockSpec(memory_space=pltpu.VMEM)
    return pl.pallas_call(
        body,
        out_shape=outs,
        in_specs=[
            pl.BlockSpec(memory_space=(spaces or {}).get(k, pltpu.VMEM))
            for k in range(len(operands))
        ],
        out_specs=jax.tree.map(lambda _: vmem, outs),
        scratch_shapes=scratch,
        compiler_params=pltpu.CompilerParams(vmem_limit_bytes=32 * 1024 * 1024),
        cost_estimate=pl.CostEstimate(flops=flops, bytes_accessed=4_000_000, transcendentals=0),
    )(*operands)


def per_device(volume, weight, cotangent):
    channels, z_cells, y_cells, x_cells = volume.shape
    slabs, pencils = lax.axis_size("sp"), lax.axis_size("gz")
    width = channels // GROUPS
    out_channels = weight.shape[4]
    out_z, out_y, out_x = cotangent.shape[1:]
    lines = z_cells * y_cells
    cells = out_y * out_x
    out_cells = slabs * pencils * out_z * out_y * out_x
    parts = 2 * pencils
    rows = 27 * width
    each = rows // 2 // parts
    padded = (each + 8) // 8 * 8
    shape = jax.ShapeDtypeStruct

    up_z = shifted(cotangent, -1, 0)
    up_c = shifted(cotangent, -1, -1)
    up_y = shifted(cotangent, 0, -1)
    classes, own = call(
        lay_out_body,
        (shape((8, channels, cells), BF), shape((out_y, channels, x_cells), BF)),
        (volume, cotangent),
        [],
        0,
    )
    share = shape((parts, padded, out_channels), F32)
    cots, keep, send = call(
        kernel_grad_body,
        (shape((2 * (out_y + 1), channels, x_cells), BF), share, share),
        (classes, own, up_z, up_y, up_c),
        [pltpu.VMEM((8, channels, cells), BF), pltpu.VMEM((rows, out_channels), F32)],
        500000000,
    )
    plane, send = in_order(classes[4:], send)
    from_z = shifted(plane, 1, 0)
    got = swapped(send, 1)
    weights = weight.reshape(27, width, out_channels)
    spread = pltpu.VMEM((27 * channels, out_channels), BF)
    volume_grad = call(
        backward_body,
        shape(volume.shape, BF),
        (cots, weights),
        [
            spread,
            pltpu.VMEM((8, channels, cells), BF),
            pltpu.VMEM((lines, channels, x_cells), BF),
        ],
        1_000_000_000,
    )
    total, level = sum_over_plane(keep, got, each, parts)
    total, volume_grad = in_order(total, volume_grad)
    total, from_z = in_order(total, from_z)
    edge = jnp.concatenate([from_z[2:], classes[2:4], classes[6:]], axis=0)[:, :, cells - out_x :]
    from_y = shifted(edge, 0, 1)
    total, level = sum_over_lines(total, level, each)
    mine = spread_over_plane(total, level, each, parts)
    output = call(
        forward_body,
        shape(cotangent.shape, BF),
        (classes, from_z, from_y, weights),
        [spread, pltpu.VMEM((27 * channels, cells), BF)],
        1_000_000_000,
    )
    mine, output = in_order(mine, output)
    other = swapped(jnp.stack(mine), 1)
    kernel_grad = None
    for side, half in enumerate((mine, other)):
        slots = [slot.astype(F32) for slot in half]
        kernel_grad = pl.pallas_call(
            functools.partial(assemble_body, 1.0 / math.sqrt(out_cells), side, parts, each),
            out_shape=shape((rows, out_channels), F32),
            in_specs=[pl.BlockSpec(memory_space=pltpu.VMEM)] * parts
            + [pl.BlockSpec(memory_space=pl.ANY)] * side,
            out_specs=pl.BlockSpec(memory_space=pl.ANY),
            scratch_shapes=[
                pltpu.VMEM((parts, each, out_channels), F32),
                pltpu.VMEM((rows // 2, out_channels), F32),
                pltpu.SemaphoreType.DMA((parts,)),
            ],
            input_output_aliases={parts: 0} if side else {},
            compiler_params=pltpu.CompilerParams(vmem_limit_bytes=32 * 1024 * 1024),
            cost_estimate=pl.CostEstimate(flops=1_000_000, bytes_accessed=1_000_000, transcendentals=0),
        )(*slots, *([kernel_grad] * side))
    kernel_grad = kernel_grad.reshape(weight.shape)
    return (output, volume_grad, kernel_grad)


def solution(mesh):
    in_specs = (P(None, "sp", "gz", None), P(), P(None, "sp", "gz", None))
    out_specs = (P(None, "sp", "gz", None), P(None, "sp", "gz", None), P())
    return jax.shard_map(
        per_device, mesh=mesh, in_specs=in_specs, out_specs=out_specs, check_vma=False
    )
```

```python
import functools
import math

import jax
import jax.numpy as jnp
from jax import lax
from jax.experimental import pallas as pl
from jax.experimental.pallas import tpu as pltpu
from jax.sharding import PartitionSpec as P

GROUPS = 2
BF = jnp.bfloat16
F32 = jnp.float32
F16 = jnp.float16


def dot(left, right, dims=((1,), (0,))):
    return lax.dot_general(left, right, (dims, ((), ())), preferred_element_type=F32)


def exact(left, right):
    return dot(left, right).astype(BF)


def ones_where(shape, condition):
    row = lax.broadcasted_iota(jnp.int32, shape, 0)
    col = lax.broadcasted_iota(jnp.int32, shape, 1)
    return jnp.where(condition(row, col), 1.0, 0.0).astype(BF)


def rows_grouped(block, inner):
    size = block * inner
    return ones_where((size, size), lambda row, col: col == (row % block) * inner + row // block)


def rows_interleaved(block, inner):
    size = block * inner
    return ones_where((size, size), lambda row, col: row == (col % block) * inner + col // block)


def taps_of(parity):
    return (1,) if parity == 0 else (0, 2)


def cotangent_rows(source_ref, count):
    channels, _, out_y, out_x = source_ref.shape
    by_row = rows_grouped(channels, out_y)
    return exact(by_row[: count * channels], source_ref[...].reshape(channels * out_y, out_x))


def place():
    at_z, at_y = lax.axis_index("sp"), lax.axis_index("gz")
    return at_z % 2, at_z // 2 % 2 * lax.axis_size("gz") + at_y


def kept(array, flag):
    return jnp.where(flag != 0, array, jnp.zeros_like(array))


def put_rows(rows, cots_ref, first):
    _, channels, x_cells = cots_ref.shape
    out_x = x_cells // 2
    both = exact(
        rows,
        ones_where(
            (out_x, x_cells),
            lambda row, col: row == jnp.where(col < out_x, col, col - out_x + 1),
        ),
    )
    for k in range(rows.shape[0] // channels):
        cots_ref[first + k] = both[k * channels : (k + 1) * channels]


def lay_out_body(vol_ref, own_ref, class_ref, cots_ref):
    channels, z_cells, y_cells, x_cells = vol_ref.shape
    out_x = x_cells // 2
    lines = z_cells * y_cells
    block = 256 // lines
    put_rows(cotangent_rows(own_ref, cots_ref.shape[0]), cots_ref, 0)
    by_line = rows_grouped(block, lines)
    halves = ones_where(
        (x_cells, x_cells),
        lambda row, col: row == jnp.where(col < out_x, 2 * col, 2 * (col - out_x) + 1),
    )
    for at in range(0, channels, block):
        rows = vol_ref[at : at + block].reshape(block * lines, x_cells)
        rows = exact(exact(by_line, rows), halves)
        for z in range(z_cells):
            for y in range(y_cells):
                k = z * y_cells + y
                line = rows[k * block : (k + 1) * block]
                for x_par in range(2):
                    class_ref[
                        (z * 2 + y % 2) * 2 + x_par,
                        at : at + block,
                        y // 2 * out_x : (y // 2 + 1) * out_x,
                    ] = line[:, x_par * out_x : (x_par + 1) * out_x]


def kernel_grad_body(
    class_ref, own_ref, up_z_ref, up_y_ref, up_c_ref,
    cots_ref, keep_ref, send_ref, shift_ref, grad_ref,
):
    out_y, channels, _ = own_ref.shape
    width = channels // GROUPS

    cots_ref[:out_y] = own_ref[...]
    next_z = (lax.axis_index("sp") < lax.axis_size("sp") - 1) * 1
    next_y = (lax.axis_index("gz") < lax.axis_size("gz") - 1) * 1
    put_rows(kept(cotangent_rows(up_y_ref, 1), next_y), cots_ref, out_y)
    put_rows(kept(cotangent_rows(up_z_ref, out_y), next_z), cots_ref, out_y + 1)
    put_rows(kept(cotangent_rows(up_c_ref, 1), next_z * next_y), cots_ref, 2 * out_y + 1)
    pair_rows(cots_ref, shift_ref)

    first_half = lax.broadcasted_iota(jnp.int32, (width, channels), 1) < width
    for a in range(3):
        for b in range(3):
            for c in range(3):
                which = ((a != 1) * 2 + (b != 1)) * 2 + (c != 1)
                cot = ((a == 0) * 2 + (b == 0)) * 2 + (c == 0)
                full = dot(class_ref[which], shift_ref[cot], ((1,), (1,)))
                tap = (a * 3 + b) * 3 + c
                grad_ref[tap * width : (tap + 1) * width] = jnp.where(
                    first_half, full[:width], full[width:]
                )

    parts, padded, _ = keep_ref.shape
    half = grad_ref.shape[0] // 2
    each = half // parts
    top = jnp.maximum(jnp.max(jnp.abs(grad_ref[...])), 1e-30)
    level = jnp.floor(jnp.log2(jnp.full((padded - each, channels), top, F32))) - 14.0
    core, at = place()
    low = core == 0
    for part in range(parts):
        slot = at ^ part
        here = grad_ref[part * each : (part + 1) * each]
        there = grad_ref[half + part * each : half + (part + 1) * each]
        keep_ref[slot, :each] = jnp.where(low, here, there)
        send_ref[slot, :each] = jnp.where(low, there, here)
        keep_ref[slot, each:] = level
        send_ref[slot, each:] = level


def pair_rows(cots_ref, shift_ref):
    out_y = cots_ref.shape[0] // 2 - 1
    out_x = cots_ref.shape[2] // 2
    for plane in range(2):
        for off in range(2):
            for step in range(2):
                for y in range(out_y):
                    shift_ref[(plane * 2 + off) * 2 + step, :, y * out_x : (y + 1) * out_x] = cots_ref[
                        plane * (out_y + 1) + off + y, :, step * out_x : (step + 1) * out_x
                    ]


def spread_groups(weight_ref, spread_ref):
    _, width, channels = weight_ref.shape
    first_half = lax.broadcasted_iota(jnp.int32, (width, channels), 1) < width
    for tap in range(27):
        part = weight_ref[tap]
        zero = jnp.zeros_like(part)
        spread_ref[tap * channels : tap * channels + width] = jnp.where(first_half, part, zero)
        spread_ref[tap * channels + width : (tap + 1) * channels] = jnp.where(first_half, zero, part)


def forward_body(class_ref, from_z_ref, from_y_ref, weight_ref, out_ref, spread_ref, patch_ref):
    _, channels, cells = class_ref.shape
    out_x = from_y_ref.shape[2]
    out_y = cells // out_x
    spread_groups(weight_ref, spread_ref)
    moved = ones_where((out_x, out_x), lambda row, col: row == col - 1)

    def piece(a, q, x_par):
        if q < 0:
            return from_y_ref[a * 2 + x_par]
        lanes = slice(q // 2 * out_x, (q // 2 + 1) * out_x)
        if a == 0:
            return from_z_ref[q % 2 * 2 + x_par, :, lanes]
        return class_ref[((a - 1) * 2 + q % 2) * 2 + x_par, :, lanes]

    for a in range(3):
        for q in range(-1, 2 * out_y):
            odd = piece(a, q, 1)
            pieces = (exact(odd, moved), piece(a, q, 0), odd)
            for b in taps_of(q % 2):
                y = (q + 1 - b) // 2
                if 0 <= y < out_y:
                    for c in range(3):
                        tap = (a * 3 + b) * 3 + c
                        patch_ref[
                            tap * channels : (tap + 1) * channels, y * out_x : (y + 1) * out_x
                        ] = pieces[c]

    @pl.when(lax.axis_index("sp") == 0)
    def _():
        patch_ref[: 9 * channels] = jnp.zeros_like(patch_ref[: 9 * channels])

    @pl.when(lax.axis_index("gz") == 0)
    def _():
        for a in range(3):
            at = a * 9 * channels
            first = patch_ref.at[at : at + 3 * channels, :out_x]
            first[...] = jnp.zeros_like(first)

    result = dot(spread_ref[...], patch_ref[...], ((0,), (0,))).astype(BF)
    stacked = jnp.concatenate(
        [result[:, y * out_x : (y + 1) * out_x] for y in range(out_y)], axis=0
    )
    out_ref[...] = exact(rows_interleaved(channels, out_y), stacked).reshape(out_ref.shape)


def backward_body(cots_ref, weight_ref, grad_ref, spread_ref, shift_ref, lines_ref):
    channels, z_cells, y_cells, x_cells = grad_ref.shape
    lines = z_cells * y_cells
    out_x = x_cells // 2
    out_y = y_cells // 2
    spread_groups(weight_ref, spread_ref)
    pair_rows(cots_ref, shift_ref)

    for z in range(z_cells):
        for y_par in range(2):
            for x_par in range(2):
                total = jnp.zeros((channels, out_y * out_x), F32)
                for a in taps_of(z):
                    for b in taps_of(y_par):
                        for c in taps_of(x_par):
                            tap = (a * 3 + b) * 3 + c
                            cot = ((a == 0) * 2 + (b == 0)) * 2 + (c == 0)
                            total += dot(
                                spread_ref[tap * channels : (tap + 1) * channels], shift_ref[cot]
                            )
                total = total.astype(BF)
                for y in range(out_y):
                    lines_ref[
                        z * y_cells + 2 * y + y_par, :, x_par * out_x : (x_par + 1) * out_x
                    ] = total[:, y * out_x : (y + 1) * out_x]
    block = 256 // lines
    by_cell = rows_interleaved(block, lines)
    joined = ones_where(
        (x_cells, x_cells),
        lambda row, col: col == jnp.where(row < out_x, 2 * row, 2 * (row - out_x) + 1),
    )
    for at in range(0, channels, block):
        rows = jnp.concatenate([lines_ref[k, at : at + block, :] for k in range(lines)], axis=0)
        rows = exact(by_cell, exact(rows, joined))
        grad_ref[at : at + block] = rows.reshape(block, z_cells, y_cells, x_cells)


def assemble_body(scale, side, parts, each, *refs):
    slots, (out_ref, held_ref, half_ref, done) = refs[:parts], refs[-4:]
    core, mine = place()
    for k, slot_ref in enumerate(slots):
        held_ref[k] = slot_ref[:each] * (jnp.exp2(slot_ref[each : each + 1]) * scale)
    rows = parts * each
    start = (core ^ side) * rows
    split = parts if each % 8 == 0 else 1
    copies = []
    for at in range(0, rows, rows // split):
        for part in range(at // each, (at + rows // split) // each):
            half_ref[part * each : (part + 1) * each] = held_ref[mine ^ part]
        copies.append(
            pltpu.make_async_copy(
                half_ref.at[pl.ds(at, rows // split)],
                out_ref.at[pl.ds(pl.multiple_of(start + at, 8), rows // split)],
                done.at[len(copies)],
            )
        )
        copies[-1].start()
    for copy in copies:
        copy.wait()


def shifted(array, by_z, by_y):
    size_z, size_y = lax.axis_size("sp"), lax.axis_size("gz")
    pairs = [
        (z * size_y + y, (z + by_z) % size_z * size_y + (y + by_y) % size_y)
        for z in range(size_z)
        for y in range(size_y)
    ]
    return lax.ppermute(array, ("sp", "gz"), pairs)


def swapped(array, flip):
    return lax.ppermute(array, "sp", [(i, i ^ flip) for i in range(lax.axis_size("sp"))])


def swapped_in_plane(array, flip):
    size_z, size_y = lax.axis_size("sp"), lax.axis_size("gz")
    pairs = []
    for z in range(size_z):
        for y in range(size_y):
            to = ((z // 2 % 2) * size_y + y) ^ flip
            to_z = z // 4 * 4 + to // size_y * 2 + z % 2
            pairs.append((z * size_y + y, to_z * size_y + to % size_y))
    return lax.ppermute(array, ("sp", "gz"), pairs)


def coded(values, level, each):
    row = lax.broadcasted_iota(jnp.int32, values.shape, values.ndim - 2)
    return jnp.where(row < each, values * jnp.exp2(-level), level).astype(F16)


def decoded(message, each):
    message = message.astype(F32)
    level = message[..., each : each + 1, :]
    return message * jnp.exp2(level), level


def in_order(*arrays):
    return lax.optimization_barrier(arrays)


def partners(parts):
    return sorted(range(1, parts), key=lambda k: -bin(k).count("1"))


def sum_over_plane(keep, got, each, parts):
    got, level = decoded(got, each)
    level = jnp.maximum(keep[0, each : each + 1], level[0]) + 1.0
    parts_got = {
        k: swapped_in_plane(coded(keep[k] + got[k], level, each), k) for k in partners(parts)
    }
    total = keep[0] + got[0]
    for k in partners(parts):
        values, its_level = decoded(parts_got[k], each)
        total = total + values
        level = jnp.maximum(level, its_level)
    return total, level + math.ceil(math.log2(parts))


def sum_over_lines(total, level, each):
    quads = lax.axis_size("sp") // 4
    message = coded(total, level, each)
    others = {k: swapped(message, 4 * k) for k in range(1, quads)}
    terms = [decoded(message, each)] + [decoded(others[k], each) for k in range(1, quads)]
    while len(terms) > 1:
        terms = [
            (left[0] + right[0], jnp.maximum(left[1], right[1]) + 1.0)
            for left, right in zip(terms[::2], terms[1::2])
        ]
    return terms[0]


def spread_over_plane(total, level, each, parts):
    message = coded(total, level, each)
    slots = {k: swapped_in_plane(message, k) for k in partners(parts)}
    slots[0] = message
    return [slots[k] for k in range(parts)]


def call(body, outs, operands, scratch=(), flops=1_000_000, spaces=None):
    vmem = pl.BlockSpec(memory_space=pltpu.VMEM)
    return pl.pallas_call(
        body,
        out_shape=outs,
        in_specs=[
            pl.BlockSpec(memory_space=(spaces or {}).get(k, pltpu.VMEM))
            for k in range(len(operands))
        ],
        out_specs=jax.tree.map(lambda _: vmem, outs),
        scratch_shapes=scratch,
        compiler_params=pltpu.CompilerParams(vmem_limit_bytes=32 * 1024 * 1024),
        cost_estimate=pl.CostEstimate(flops=flops, bytes_accessed=4_000_000, transcendentals=0),
    )(*operands)


def per_device(volume, weight, cotangent):
    channels, z_cells, y_cells, x_cells = volume.shape
    slabs, pencils = lax.axis_size("sp"), lax.axis_size("gz")
    width = channels // GROUPS
    out_channels = weight.shape[4]
    out_z, out_y, out_x = cotangent.shape[1:]
    lines = z_cells * y_cells
    cells = out_y * out_x
    out_cells = slabs * pencils * out_z * out_y * out_x
    parts = 2 * pencils
    rows = 27 * width
    each = rows // 2 // parts
    padded = (each + 8) // 8 * 8
    shape = jax.ShapeDtypeStruct

    up_z = shifted(cotangent, -1, 0)
    up_c = shifted(cotangent, -1, -1)
    up_y = shifted(cotangent, 0, -1)
    classes, own = call(
        lay_out_body,
        (shape((8, channels, cells), BF), shape((out_y, channels, x_cells), BF)),
        (volume, cotangent),
        [],
        0,
    )
    share = shape((parts, padded, out_channels), F32)
    cots, keep, send = call(
        kernel_grad_body,
        (shape((2 * (out_y + 1), channels, x_cells), BF), share, share),
        (classes, own, up_z, up_y, up_c),
        [pltpu.VMEM((8, channels, cells), BF), pltpu.VMEM((rows, out_channels), F32)],
        500000000,
    )
    from_z = shifted(classes[4:], 1, 0)
    got = swapped(coded(send, send[0, each : each + 1], each), 1)
    weights = weight.reshape(27, width, out_channels)
    spread = pltpu.VMEM((27 * channels, out_channels), BF)
    volume_grad = call(
        backward_body,
        shape(volume.shape, BF),
        (cots, weights),
        [
            spread,
            pltpu.VMEM((8, channels, cells), BF),
            pltpu.VMEM((lines, channels, x_cells), BF),
        ],
        1_000_000_000,
    )
    total, level = sum_over_plane(keep, got, each, parts)
    total, volume_grad = in_order(total, volume_grad)
    total, from_z = in_order(total, from_z)
    edge = jnp.concatenate([from_z[2:], classes[2:4], classes[6:]], axis=0)[:, :, cells - out_x :]
    from_y = shifted(edge, 0, 1)
    total, level = sum_over_lines(total, level, each)
    mine = spread_over_plane(total, level, each, parts)
    output = call(
        forward_body,
        shape(cotangent.shape, BF),
        (classes, from_z, from_y, weights),
        [spread, pltpu.VMEM((27 * channels, cells), BF)],
        1_000_000_000,
    )
    mine, output = in_order(mine, output)
    other = swapped(jnp.stack(mine), 1)
    kernel_grad = None
    for side, half in enumerate((mine, other)):
        slots = [slot.astype(F32) for slot in half]
        kernel_grad = pl.pallas_call(
            functools.partial(assemble_body, 1.0 / math.sqrt(out_cells), side, parts, each),
            out_shape=shape((rows, out_channels), F32),
            in_specs=[pl.BlockSpec(memory_space=pltpu.VMEM)] * parts
            + [pl.BlockSpec(memory_space=pl.ANY)] * side,
            out_specs=pl.BlockSpec(memory_space=pl.ANY),
            scratch_shapes=[
                pltpu.VMEM((parts, each, out_channels), F32),
                pltpu.VMEM((rows // 2, out_channels), F32),
                pltpu.SemaphoreType.DMA((parts,)),
            ],
            input_output_aliases={parts: 0} if side else {},
            compiler_params=pltpu.CompilerParams(vmem_limit_bytes=32 * 1024 * 1024),
            cost_estimate=pl.CostEstimate(flops=1_000_000, bytes_accessed=1_000_000, transcendentals=0),
        )(*slots, *([kernel_grad] * side))
    kernel_grad = kernel_grad.reshape(weight.shape)
    return (output, volume_grad, kernel_grad)


def solution(mesh):
    in_specs = (P(None, "sp", "gz", None), P(), P(None, "sp", "gz", None))
    out_specs = (P(None, "sp", "gz", None), P(None, "sp", "gz", None), P())
    return jax.shard_map(
        per_device, mesh=mesh, in_specs=in_specs, out_specs=out_specs, check_vma=False
    )
```

```python
import functools
import math

import jax
import jax.numpy as jnp
from jax import lax
from jax.experimental import pallas as pl
from jax.experimental.pallas import tpu as pltpu
from jax.sharding import PartitionSpec as P

GROUPS = 2
BF = jnp.bfloat16
F32 = jnp.float32
F16 = jnp.float16


def dot(left, right, dims=((1,), (0,))):
    return lax.dot_general(left, right, (dims, ((), ())), preferred_element_type=F32)


def exact(left, right):
    return dot(left, right).astype(BF)


def ones_where(shape, condition):
    row = lax.broadcasted_iota(jnp.int32, shape, 0)
    col = lax.broadcasted_iota(jnp.int32, shape, 1)
    return jnp.where(condition(row, col), 1.0, 0.0).astype(BF)


def rows_grouped(block, inner):
    size = block * inner
    return ones_where((size, size), lambda row, col: col == (row % block) * inner + row // block)


def rows_interleaved(block, inner):
    size = block * inner
    return ones_where((size, size), lambda row, col: row == (col % block) * inner + col // block)


def taps_of(parity):
    return (1,) if parity == 0 else (0, 2)


def cotangent_rows(source_ref, count):
    channels, _, out_y, out_x = source_ref.shape
    by_row = rows_grouped(channels, out_y)
    return exact(by_row[: count * channels], source_ref[...].reshape(channels * out_y, out_x))


def place():
    at_z, at_y = lax.axis_index("sp"), lax.axis_index("gz")
    return at_z % 2, at_z // 2 % 2 * lax.axis_size("gz") + at_y


def kept(array, flag):
    return jnp.where(flag != 0, array, jnp.zeros_like(array))


def put_rows(rows, cots_ref, first):
    _, channels, x_cells = cots_ref.shape
    out_x = x_cells // 2
    both = exact(
        rows,
        ones_where(
            (out_x, x_cells),
            lambda row, col: row == jnp.where(col < out_x, col, col - out_x + 1),
        ),
    )
    for k in range(rows.shape[0] // channels):
        cots_ref[first + k] = both[k * channels : (k + 1) * channels]


def near_taps():
    return [(a, b, c) for a in (1, 2) for b in (1, 2) for c in range(3)]


def lay_out_body(vol_ref, own_ref, class_ref, cots_ref, near_ref):
    channels, z_cells, y_cells, x_cells = vol_ref.shape
    out_x = x_cells // 2
    lines = z_cells * y_cells
    block = 256 // lines
    put_rows(cotangent_rows(own_ref, cots_ref.shape[0]), cots_ref, 0)
    by_line = rows_grouped(block, lines)
    halves = ones_where(
        (x_cells, x_cells),
        lambda row, col: row == jnp.where(col < out_x, 2 * col, 2 * (col - out_x) + 1),
    )
    for at in range(0, channels, block):
        rows = vol_ref[at : at + block].reshape(block * lines, x_cells)
        rows = exact(exact(by_line, rows), halves)
        for z in range(z_cells):
            for y in range(y_cells):
                k = z * y_cells + y
                line = rows[k * block : (k + 1) * block]
                for x_par in range(2):
                    class_ref[
                        (z * 2 + y % 2) * 2 + x_par,
                        at : at + block,
                        y // 2 * out_x : (y // 2 + 1) * out_x,
                    ] = line[:, x_par * out_x : (x_par + 1) * out_x]

    out_y = cots_ref.shape[0]
    width = channels // GROUPS
    first_half = lax.broadcasted_iota(jnp.int32, (width, channels), 1) < width
    pairs = [
        jnp.concatenate(
            [cots_ref[y, :, step * out_x : (step + 1) * out_x] for y in range(out_y)], axis=1
        )
        for step in range(2)
    ]
    for n, (a, b, c) in enumerate(near_taps()):
        full = dot(
            class_ref[((a != 1) * 2 + (b != 1)) * 2 + (c != 1)], pairs[int(c == 0)], ((1,), (1,))
        )
        near_ref[n * width : (n + 1) * width] = jnp.where(first_half, full[:width], full[width:])


def kernel_grad_body(
    class_ref, own_ref, near_ref, up_z_ref, up_y_ref, up_c_ref,
    cots_ref, keep_ref, send_ref, shift_ref, grad_ref,
):
    out_y, channels, _ = own_ref.shape
    width = channels // GROUPS

    cots_ref[:out_y] = own_ref[...]
    next_z = (lax.axis_index("sp") < lax.axis_size("sp") - 1) * 1
    next_y = (lax.axis_index("gz") < lax.axis_size("gz") - 1) * 1
    put_rows(kept(cotangent_rows(up_y_ref, 1), next_y), cots_ref, out_y)
    put_rows(kept(cotangent_rows(up_z_ref, out_y), next_z), cots_ref, out_y + 1)
    put_rows(kept(cotangent_rows(up_c_ref, 1), next_z * next_y), cots_ref, 2 * out_y + 1)
    pair_rows(cots_ref, shift_ref)

    first_half = lax.broadcasted_iota(jnp.int32, (width, channels), 1) < width
    for a in range(3):
        for b in range(3):
            for c in range(3):
                which = ((a != 1) * 2 + (b != 1)) * 2 + (c != 1)
                cot = ((a == 0) * 2 + (b == 0)) * 2 + (c == 0)
                if (a, b, c) in near_taps():
                    at = near_taps().index((a, b, c)) * width
                    tap = (a * 3 + b) * 3 + c
                    grad_ref[tap * width : (tap + 1) * width] = near_ref[at : at + width]
                    continue
                full = dot(class_ref[which], shift_ref[cot], ((1,), (1,)))
                tap = (a * 3 + b) * 3 + c
                grad_ref[tap * width : (tap + 1) * width] = jnp.where(
                    first_half, full[:width], full[width:]
                )

    parts, padded, _ = keep_ref.shape
    half = grad_ref.shape[0] // 2
    each = half // parts
    top = jnp.maximum(jnp.max(jnp.abs(grad_ref[...])), 1e-30)
    level = jnp.floor(jnp.log2(jnp.full((padded - each, channels), top, F32))) - 14.0
    core, at = place()
    low = core == 0
    for part in range(parts):
        slot = at ^ part
        here = grad_ref[part * each : (part + 1) * each]
        there = grad_ref[half + part * each : half + (part + 1) * each]
        keep_ref[slot, :each] = jnp.where(low, here, there)
        send_ref[slot, :each] = jnp.where(low, there, here)
        keep_ref[slot, each:] = level
        send_ref[slot, each:] = level


def pair_rows(cots_ref, shift_ref):
    out_y = cots_ref.shape[0] // 2 - 1
    out_x = cots_ref.shape[2] // 2
    for plane in range(2):
        for off in range(2):
            for step in range(2):
                for y in range(out_y):
                    shift_ref[(plane * 2 + off) * 2 + step, :, y * out_x : (y + 1) * out_x] = cots_ref[
                        plane * (out_y + 1) + off + y, :, step * out_x : (step + 1) * out_x
                    ]


def spread_groups(weight_ref, spread_ref):
    _, width, channels = weight_ref.shape
    first_half = lax.broadcasted_iota(jnp.int32, (width, channels), 1) < width
    for tap in range(27):
        part = weight_ref[tap]
        zero = jnp.zeros_like(part)
        spread_ref[tap * channels : tap * channels + width] = jnp.where(first_half, part, zero)
        spread_ref[tap * channels + width : (tap + 1) * channels] = jnp.where(first_half, zero, part)


def forward_body(class_ref, from_z_ref, from_y_ref, weight_ref, out_ref, spread_ref, patch_ref):
    _, channels, cells = class_ref.shape
    out_x = from_y_ref.shape[2]
    out_y = cells // out_x
    spread_groups(weight_ref, spread_ref)
    moved = ones_where((out_x, out_x), lambda row, col: row == col - 1)

    def piece(a, q, x_par):
        if q < 0:
            return from_y_ref[a * 2 + x_par]
        lanes = slice(q // 2 * out_x, (q // 2 + 1) * out_x)
        if a == 0:
            return from_z_ref[q % 2 * 2 + x_par, :, lanes]
        return class_ref[((a - 1) * 2 + q % 2) * 2 + x_par, :, lanes]

    for a in range(3):
        for q in range(-1, 2 * out_y):
            odd = piece(a, q, 1)
            pieces = (exact(odd, moved), piece(a, q, 0), odd)
            for b in taps_of(q % 2):
                y = (q + 1 - b) // 2
                if 0 <= y < out_y:
                    for c in range(3):
                        tap = (a * 3 + b) * 3 + c
                        patch_ref[
                            tap * channels : (tap + 1) * channels, y * out_x : (y + 1) * out_x
                        ] = pieces[c]

    @pl.when(lax.axis_index("sp") == 0)
    def _():
        patch_ref[: 9 * channels] = jnp.zeros_like(patch_ref[: 9 * channels])

    @pl.when(lax.axis_index("gz") == 0)
    def _():
        for a in range(3):
            at = a * 9 * channels
            first = patch_ref.at[at : at + 3 * channels, :out_x]
            first[...] = jnp.zeros_like(first)

    result = dot(spread_ref[...], patch_ref[...], ((0,), (0,))).astype(BF)
    stacked = jnp.concatenate(
        [result[:, y * out_x : (y + 1) * out_x] for y in range(out_y)], axis=0
    )
    out_ref[...] = exact(rows_interleaved(channels, out_y), stacked).reshape(out_ref.shape)


def backward_body(cots_ref, weight_ref, grad_ref, spread_ref, shift_ref, lines_ref):
    channels, z_cells, y_cells, x_cells = grad_ref.shape
    lines = z_cells * y_cells
    out_x = x_cells // 2
    out_y = y_cells // 2
    spread_groups(weight_ref, spread_ref)
    pair_rows(cots_ref, shift_ref)

    for z in range(z_cells):
        for y_par in range(2):
            for x_par in range(2):
                total = jnp.zeros((channels, out_y * out_x), F32)
                for a in taps_of(z):
                    for b in taps_of(y_par):
                        for c in taps_of(x_par):
                            tap = (a * 3 + b) * 3 + c
                            cot = ((a == 0) * 2 + (b == 0)) * 2 + (c == 0)
                            total += dot(
                                spread_ref[tap * channels : (tap + 1) * channels], shift_ref[cot]
                            )
                total = total.astype(BF)
                for y in range(out_y):
                    lines_ref[
                        z * y_cells + 2 * y + y_par, :, x_par * out_x : (x_par + 1) * out_x
                    ] = total[:, y * out_x : (y + 1) * out_x]
    block = 256 // lines
    by_cell = rows_interleaved(block, lines)
    joined = ones_where(
        (x_cells, x_cells),
        lambda row, col: col == jnp.where(row < out_x, 2 * row, 2 * (row - out_x) + 1),
    )
    for at in range(0, channels, block):
        rows = jnp.concatenate([lines_ref[k, at : at + block, :] for k in range(lines)], axis=0)
        rows = exact(by_cell, exact(rows, joined))
        grad_ref[at : at + block] = rows.reshape(block, z_cells, y_cells, x_cells)


def assemble_body(scale, side, parts, each, *refs):
    slots, (out_ref, held_ref, half_ref, done) = refs[:parts], refs[-4:]
    core, mine = place()
    for k, slot_ref in enumerate(slots):
        held_ref[k] = slot_ref[:each] * (jnp.exp2(slot_ref[each : each + 1]) * scale)
    rows = parts * each
    start = (core ^ side) * rows
    split = parts if each % 8 == 0 else 1
    copies = []
    for at in range(0, rows, rows // split):
        for part in range(at // each, (at + rows // split) // each):
            half_ref[part * each : (part + 1) * each] = held_ref[mine ^ part]
        copies.append(
            pltpu.make_async_copy(
                half_ref.at[pl.ds(at, rows // split)],
                out_ref.at[pl.ds(pl.multiple_of(start + at, 8), rows // split)],
                done.at[len(copies)],
            )
        )
        copies[-1].start()
    for copy in copies:
        copy.wait()


def shifted(array, by_z, by_y):
    size_z, size_y = lax.axis_size("sp"), lax.axis_size("gz")
    pairs = [
        (z * size_y + y, (z + by_z) % size_z * size_y + (y + by_y) % size_y)
        for z in range(size_z)
        for y in range(size_y)
    ]
    return lax.ppermute(array, ("sp", "gz"), pairs)


def swapped(array, flip):
    return lax.ppermute(array, "sp", [(i, i ^ flip) for i in range(lax.axis_size("sp"))])


def swapped_in_plane(array, flip):
    size_z, size_y = lax.axis_size("sp"), lax.axis_size("gz")
    pairs = []
    for z in range(size_z):
        for y in range(size_y):
            to = ((z // 2 % 2) * size_y + y) ^ flip
            to_z = z // 4 * 4 + to // size_y * 2 + z % 2
            pairs.append((z * size_y + y, to_z * size_y + to % size_y))
    return lax.ppermute(array, ("sp", "gz"), pairs)


def coded(values, level, each):
    row = lax.broadcasted_iota(jnp.int32, values.shape, values.ndim - 2)
    return jnp.where(row < each, values * jnp.exp2(-level), level).astype(F16)


def decoded(message, each):
    message = message.astype(F32)
    level = message[..., each : each + 1, :]
    return message * jnp.exp2(level), level


def in_order(*arrays):
    return lax.optimization_barrier(arrays)


def partners(parts):
    return sorted(range(1, parts), key=lambda k: -bin(k).count("1"))


def sum_over_plane(keep, got, each, parts):
    got, level = decoded(got, each)
    level = jnp.maximum(keep[0, each : each + 1], level[0]) + 1.0
    parts_got = {
        k: swapped_in_plane(coded(keep[k] + got[k], level, each), k) for k in partners(parts)
    }
    total = keep[0] + got[0]
    for k in partners(parts):
        values, its_level = decoded(parts_got[k], each)
        total = total + values
        level = jnp.maximum(level, its_level)
    return total, level + math.ceil(math.log2(parts))


def sum_over_lines(total, level, each):
    quads = lax.axis_size("sp") // 4
    message = coded(total, level, each)
    others = {k: swapped(message, 4 * k) for k in range(1, quads)}
    terms = [decoded(message, each)] + [decoded(others[k], each) for k in range(1, quads)]
    while len(terms) > 1:
        terms = [
            (left[0] + right[0], jnp.maximum(left[1], right[1]) + 1.0)
            for left, right in zip(terms[::2], terms[1::2])
        ]
    return terms[0]


def spread_over_plane(total, level, each, parts):
    message = coded(total, level, each)
    slots = {k: swapped_in_plane(message, k) for k in partners(parts)}
    slots[0] = message
    return [slots[k] for k in range(parts)]


def call(body, outs, operands, scratch=(), flops=1_000_000, spaces=None):
    vmem = pl.BlockSpec(memory_space=pltpu.VMEM)
    return pl.pallas_call(
        body,
        out_shape=outs,
        in_specs=[
            pl.BlockSpec(memory_space=(spaces or {}).get(k, pltpu.VMEM))
            for k in range(len(operands))
        ],
        out_specs=jax.tree.map(lambda _: vmem, outs),
        scratch_shapes=scratch,
        compiler_params=pltpu.CompilerParams(vmem_limit_bytes=32 * 1024 * 1024),
        cost_estimate=pl.CostEstimate(flops=flops, bytes_accessed=4_000_000, transcendentals=0),
    )(*operands)


def per_device(volume, weight, cotangent):
    channels, z_cells, y_cells, x_cells = volume.shape
    slabs, pencils = lax.axis_size("sp"), lax.axis_size("gz")
    width = channels // GROUPS
    out_channels = weight.shape[4]
    out_z, out_y, out_x = cotangent.shape[1:]
    lines = z_cells * y_cells
    cells = out_y * out_x
    out_cells = slabs * pencils * out_z * out_y * out_x
    parts = 2 * pencils
    rows = 27 * width
    each = rows // 2 // parts
    padded = (each + 8) // 8 * 8
    shape = jax.ShapeDtypeStruct

    up_z = shifted(cotangent, -1, 0)
    up_c = shifted(cotangent, -1, -1)
    up_y = shifted(cotangent, 0, -1)
    classes, own, near = call(
        lay_out_body,
        (
            shape((8, channels, cells), BF),
            shape((out_y, channels, x_cells), BF),
            shape((len(near_taps()) * width, out_channels), F32),
        ),
        (volume, cotangent),
        [],
        0,
    )
    share = shape((parts, padded, out_channels), F32)
    cots, keep, send = call(
        kernel_grad_body,
        (shape((2 * (out_y + 1), channels, x_cells), BF), share, share),
        (classes, own, near, up_z, up_y, up_c),
        [pltpu.VMEM((8, channels, cells), BF), pltpu.VMEM((rows, out_channels), F32)],
        500000000,
    )
    from_z = shifted(classes[4:], 1, 0)
    got = swapped(coded(send, send[0, each : each + 1], each), 1)
    weights = weight.reshape(27, width, out_channels)
    spread = pltpu.VMEM((27 * channels, out_channels), BF)
    volume_grad = call(
        backward_body,
        shape(volume.shape, BF),
        (cots, weights),
        [
            spread,
            pltpu.VMEM((8, channels, cells), BF),
            pltpu.VMEM((lines, channels, x_cells), BF),
        ],
        1_000_000_000,
    )
    total, level = sum_over_plane(keep, got, each, parts)
    total, volume_grad = in_order(total, volume_grad)
    total, from_z = in_order(total, from_z)
    edge = jnp.concatenate([from_z[2:], classes[2:4], classes[6:]], axis=0)[:, :, cells - out_x :]
    from_y = shifted(edge, 0, 1)
    total, level = sum_over_lines(total, level, each)
    mine = spread_over_plane(total, level, each, parts)
    output = call(
        forward_body,
        shape(cotangent.shape, BF),
        (classes, from_z, from_y, weights),
        [spread, pltpu.VMEM((27 * channels, cells), BF)],
        1_000_000_000,
    )
    mine, output = in_order(mine, output)
    other = swapped(jnp.stack(mine), 1)
    kernel_grad = None
    for side, half in enumerate((mine, other)):
        slots = [slot.astype(F32) for slot in half]
        kernel_grad = pl.pallas_call(
            functools.partial(assemble_body, 1.0 / math.sqrt(out_cells), side, parts, each),
            out_shape=shape((rows, out_channels), F32),
            in_specs=[pl.BlockSpec(memory_space=pltpu.VMEM)] * parts
            + [pl.BlockSpec(memory_space=pl.ANY)] * side,
            out_specs=pl.BlockSpec(memory_space=pl.ANY),
            scratch_shapes=[
                pltpu.VMEM((parts, each, out_channels), F32),
                pltpu.VMEM((rows // 2, out_channels), F32),
                pltpu.SemaphoreType.DMA((parts,)),
            ],
            input_output_aliases={parts: 0} if side else {},
            compiler_params=pltpu.CompilerParams(vmem_limit_bytes=32 * 1024 * 1024),
            cost_estimate=pl.CostEstimate(flops=1_000_000, bytes_accessed=1_000_000, transcendentals=0),
        )(*slots, *([kernel_grad] * side))
    kernel_grad = kernel_grad.reshape(weight.shape)
    return (output, volume_grad, kernel_grad)


def solution(mesh):
    in_specs = (P(None, "sp", "gz", None), P(), P(None, "sp", "gz", None))
    out_specs = (P(None, "sp", "gz", None), P(None, "sp", "gz", None), P())
    return jax.shard_map(
        per_device, mesh=mesh, in_specs=in_specs, out_specs=out_specs, check_vma=False
    )
```

```python
import functools
import math

import jax
import jax.numpy as jnp
from jax import lax
from jax.experimental import pallas as pl
from jax.experimental.pallas import tpu as pltpu
from jax.sharding import PartitionSpec as P

GROUPS = 2
BF = jnp.bfloat16
F32 = jnp.float32
F16 = jnp.float16


def dot(left, right, dims=((1,), (0,))):
    return lax.dot_general(left, right, (dims, ((), ())), preferred_element_type=F32)


def exact(left, right):
    return dot(left, right).astype(BF)


def ones_where(shape, condition):
    row = lax.broadcasted_iota(jnp.int32, shape, 0)
    col = lax.broadcasted_iota(jnp.int32, shape, 1)
    return jnp.where(condition(row, col), 1.0, 0.0).astype(BF)


def rows_grouped(block, inner):
    size = block * inner
    return ones_where((size, size), lambda row, col: col == (row % block) * inner + row // block)


def rows_interleaved(block, inner):
    size = block * inner
    return ones_where((size, size), lambda row, col: row == (col % block) * inner + col // block)


def taps_of(parity):
    return (1,) if parity == 0 else (0, 2)


def cotangent_rows(source_ref, count):
    channels, _, out_y, out_x = source_ref.shape
    by_row = rows_grouped(channels, out_y)
    return exact(by_row[: count * channels], source_ref[...].reshape(channels * out_y, out_x))


def place():
    at_z, at_y = lax.axis_index("sp"), lax.axis_index("gz")
    return at_z % 2, at_z // 2 % 2 * lax.axis_size("gz") + at_y


def kept(array, flag):
    return jnp.where(flag != 0, array, jnp.zeros_like(array))


def put_rows(rows, cots_ref, first):
    _, channels, x_cells = cots_ref.shape
    out_x = x_cells // 2
    both = exact(
        rows,
        ones_where(
            (out_x, x_cells),
            lambda row, col: row == jnp.where(col < out_x, col, col - out_x + 1),
        ),
    )
    for k in range(rows.shape[0] // channels):
        cots_ref[first + k] = both[k * channels : (k + 1) * channels]


def near_taps():
    return [(a, b, c) for a in (1, 2) for b in (1, 2) for c in range(3)]


def lay_out_body(vol_ref, own_ref, class_ref, cots_ref, near_ref):
    channels, z_cells, y_cells, x_cells = vol_ref.shape
    out_x = x_cells // 2
    lines = z_cells * y_cells
    block = 256 // lines
    put_rows(cotangent_rows(own_ref, cots_ref.shape[0]), cots_ref, 0)
    by_line = rows_grouped(block, lines)
    halves = ones_where(
        (x_cells, x_cells),
        lambda row, col: row == jnp.where(col < out_x, 2 * col, 2 * (col - out_x) + 1),
    )
    for at in range(0, channels, block):
        rows = vol_ref[at : at + block].reshape(block * lines, x_cells)
        rows = exact(exact(by_line, rows), halves)
        for z in range(z_cells):
            for y in range(y_cells):
                k = z * y_cells + y
                line = rows[k * block : (k + 1) * block]
                for x_par in range(2):
                    class_ref[
                        (z * 2 + y % 2) * 2 + x_par,
                        at : at + block,
                        y // 2 * out_x : (y // 2 + 1) * out_x,
                    ] = line[:, x_par * out_x : (x_par + 1) * out_x]

    out_y = cots_ref.shape[0]
    width = channels // GROUPS
    first_half = lax.broadcasted_iota(jnp.int32, (width, channels), 1) < width
    pairs = [
        jnp.concatenate(
            [cots_ref[y, :, step * out_x : (step + 1) * out_x] for y in range(out_y)], axis=1
        )
        for step in range(2)
    ]
    for n, (a, b, c) in enumerate(near_taps()):
        full = dot(
            class_ref[((a != 1) * 2 + (b != 1)) * 2 + (c != 1)], pairs[int(c == 0)], ((1,), (1,))
        )
        near_ref[n * width : (n + 1) * width] = jnp.where(first_half, full[:width], full[width:])


def kernel_grad_body(
    class_ref, own_ref, near_ref, up_z_ref, up_y_ref, up_c_ref,
    cots_ref, keep_ref, send_ref, shift_ref, grad_ref,
):
    out_y, channels, _ = own_ref.shape
    width = channels // GROUPS

    cots_ref[:out_y] = own_ref[...]
    next_z = (lax.axis_index("sp") < lax.axis_size("sp") - 1) * 1
    next_y = (lax.axis_index("gz") < lax.axis_size("gz") - 1) * 1
    put_rows(kept(cotangent_rows(up_y_ref, 1), next_y), cots_ref, out_y)
    put_rows(kept(cotangent_rows(up_z_ref, out_y), next_z), cots_ref, out_y + 1)
    put_rows(kept(cotangent_rows(up_c_ref, 1), next_z * next_y), cots_ref, 2 * out_y + 1)
    pair_rows(cots_ref, shift_ref)

    first_half = lax.broadcasted_iota(jnp.int32, (width, channels), 1) < width
    for a in range(3):
        for b in range(3):
            for c in range(3):
                which = ((a != 1) * 2 + (b != 1)) * 2 + (c != 1)
                cot = ((a == 0) * 2 + (b == 0)) * 2 + (c == 0)
                if (a, b, c) in near_taps():
                    at = near_taps().index((a, b, c)) * width
                    tap = (a * 3 + b) * 3 + c
                    grad_ref[tap * width : (tap + 1) * width] = near_ref[at : at + width]
                    continue
                full = dot(class_ref[which], shift_ref[cot], ((1,), (1,)))
                tap = (a * 3 + b) * 3 + c
                grad_ref[tap * width : (tap + 1) * width] = jnp.where(
                    first_half, full[:width], full[width:]
                )

    parts, padded, _ = keep_ref.shape
    half = grad_ref.shape[0] // 2
    each = half // parts
    top = jnp.maximum(jnp.max(jnp.abs(grad_ref[...])), 1e-30)
    level = jnp.floor(jnp.log2(jnp.full((padded - each, channels), top, F32))) - 14.0
    core, at = place()
    low = core == 0
    for part in range(parts):
        slot = at ^ part
        here = grad_ref[part * each : (part + 1) * each]
        there = grad_ref[half + part * each : half + (part + 1) * each]
        keep_ref[slot, :each] = jnp.where(low, here, there)
        send_ref[slot, :each] = jnp.where(low, there, here)
        keep_ref[slot, each:] = level
        send_ref[slot, each:] = level


def pair_rows(cots_ref, shift_ref):
    out_y = cots_ref.shape[0] // 2 - 1
    out_x = cots_ref.shape[2] // 2
    for plane in range(2):
        for off in range(2):
            for step in range(2):
                for y in range(out_y):
                    shift_ref[(plane * 2 + off) * 2 + step, :, y * out_x : (y + 1) * out_x] = cots_ref[
                        plane * (out_y + 1) + off + y, :, step * out_x : (step + 1) * out_x
                    ]


def spread_groups(weight_ref, spread_ref):
    _, width, channels = weight_ref.shape
    first_half = lax.broadcasted_iota(jnp.int32, (width, channels), 1) < width
    for tap in range(27):
        part = weight_ref[tap]
        zero = jnp.zeros_like(part)
        spread_ref[tap * channels : tap * channels + width] = jnp.where(first_half, part, zero)
        spread_ref[tap * channels + width : (tap + 1) * channels] = jnp.where(first_half, zero, part)


def forward_body(class_ref, from_z_ref, from_y_ref, weight_ref, out_ref, spread_ref, patch_ref):
    _, channels, cells = class_ref.shape
    out_x = from_y_ref.shape[2]
    out_y = cells // out_x
    spread_groups(weight_ref, spread_ref)
    moved = ones_where((out_x, out_x), lambda row, col: row == col - 1)

    def piece(a, q, x_par):
        if q < 0:
            return from_y_ref[a * 2 + x_par]
        lanes = slice(q // 2 * out_x, (q // 2 + 1) * out_x)
        if a == 0:
            return from_z_ref[q % 2 * 2 + x_par, :, lanes]
        return class_ref[((a - 1) * 2 + q % 2) * 2 + x_par, :, lanes]

    for a in range(3):
        for q in range(-1, 2 * out_y):
            odd = piece(a, q, 1)
            pieces = (exact(odd, moved), piece(a, q, 0), odd)
            for b in taps_of(q % 2):
                y = (q + 1 - b) // 2
                if 0 <= y < out_y:
                    for c in range(3):
                        tap = (a * 3 + b) * 3 + c
                        patch_ref[
                            tap * channels : (tap + 1) * channels, y * out_x : (y + 1) * out_x
                        ] = pieces[c]

    @pl.when(lax.axis_index("sp") == 0)
    def _():
        patch_ref[: 9 * channels] = jnp.zeros_like(patch_ref[: 9 * channels])

    @pl.when(lax.axis_index("gz") == 0)
    def _():
        for a in range(3):
            at = a * 9 * channels
            first = patch_ref.at[at : at + 3 * channels, :out_x]
            first[...] = jnp.zeros_like(first)

    result = dot(spread_ref[...], patch_ref[...], ((0,), (0,))).astype(BF)
    stacked = jnp.concatenate(
        [result[:, y * out_x : (y + 1) * out_x] for y in range(out_y)], axis=0
    )
    out_ref[...] = exact(rows_interleaved(channels, out_y), stacked).reshape(out_ref.shape)


def backward_body(cots_ref, weight_ref, grad_ref, spread_ref, shift_ref, lines_ref):
    channels, z_cells, y_cells, x_cells = grad_ref.shape
    lines = z_cells * y_cells
    out_x = x_cells // 2
    out_y = y_cells // 2
    spread_groups(weight_ref, spread_ref)
    pair_rows(cots_ref, shift_ref)

    for z in range(z_cells):
        for y_par in range(2):
            for x_par in range(2):
                total = jnp.zeros((channels, out_y * out_x), F32)
                for a in taps_of(z):
                    for b in taps_of(y_par):
                        for c in taps_of(x_par):
                            tap = (a * 3 + b) * 3 + c
                            cot = ((a == 0) * 2 + (b == 0)) * 2 + (c == 0)
                            total += dot(
                                spread_ref[tap * channels : (tap + 1) * channels], shift_ref[cot]
                            )
                total = total.astype(BF)
                for y in range(out_y):
                    lines_ref[
                        z * y_cells + 2 * y + y_par, :, x_par * out_x : (x_par + 1) * out_x
                    ] = total[:, y * out_x : (y + 1) * out_x]
    block = 256 // lines
    by_cell = rows_interleaved(block, lines)
    joined = ones_where(
        (x_cells, x_cells),
        lambda row, col: col == jnp.where(row < out_x, 2 * row, 2 * (row - out_x) + 1),
    )
    for at in range(0, channels, block):
        rows = jnp.concatenate([lines_ref[k, at : at + block, :] for k in range(lines)], axis=0)
        rows = exact(by_cell, exact(rows, joined))
        grad_ref[at : at + block] = rows.reshape(block, z_cells, y_cells, x_cells)


def assemble_body(scale, side, parts, each, *refs):
    slots, (out_ref, held_ref, half_ref, done) = refs[:parts], refs[-4:]
    core, mine = place()
    for k, slot_ref in enumerate(slots):
        held_ref[k] = slot_ref[:each] * (jnp.exp2(slot_ref[each : each + 1]) * scale)
    rows = parts * each
    start = (core ^ side) * rows
    split = parts if each % 8 == 0 else 1
    copies = []
    for at in range(0, rows, rows // split):
        for part in range(at // each, (at + rows // split) // each):
            half_ref[part * each : (part + 1) * each] = held_ref[mine ^ part]
        copies.append(
            pltpu.make_async_copy(
                half_ref.at[pl.ds(at, rows // split)],
                out_ref.at[pl.ds(pl.multiple_of(start + at, 8), rows // split)],
                done.at[len(copies)],
            )
        )
        copies[-1].start()
    for copy in copies:
        copy.wait()


def shifted(array, by_z, by_y):
    size_z, size_y = lax.axis_size("sp"), lax.axis_size("gz")
    pairs = [
        (z * size_y + y, (z + by_z) % size_z * size_y + (y + by_y) % size_y)
        for z in range(size_z)
        for y in range(size_y)
    ]
    return lax.ppermute(array, ("sp", "gz"), pairs)


def swapped(array, flip):
    return lax.ppermute(array, "sp", [(i, i ^ flip) for i in range(lax.axis_size("sp"))])


def swapped_in_plane(array, flip):
    size_z, size_y = lax.axis_size("sp"), lax.axis_size("gz")
    pairs = []
    for z in range(size_z):
        for y in range(size_y):
            to = ((z // 2 % 2) * size_y + y) ^ flip
            to_z = z // 4 * 4 + to // size_y * 2 + z % 2
            pairs.append((z * size_y + y, to_z * size_y + to % size_y))
    return lax.ppermute(array, ("sp", "gz"), pairs)


def coded(values, level, each):
    row = lax.broadcasted_iota(jnp.int32, values.shape, values.ndim - 2)
    return jnp.where(row < each, values * jnp.exp2(-level), level).astype(F16)


def decoded(message, each):
    message = message.astype(F32)
    level = message[..., each : each + 1, :]
    return message * jnp.exp2(level), level


def in_order(*arrays):
    return lax.optimization_barrier(arrays)


def partners(parts):
    return sorted(range(1, parts), key=lambda k: -bin(k).count("1"))


def sum_over_plane(keep, got, each, parts):
    level = jnp.maximum(keep[0, each : each + 1], got[0, each : each + 1]) + 1.0
    parts_got = {
        k: swapped_in_plane(coded(keep[k] + got[k], level, each), k) for k in partners(parts)
    }
    total = keep[0] + got[0]
    for k in partners(parts):
        values, its_level = decoded(parts_got[k], each)
        total = total + values
        level = jnp.maximum(level, its_level)
    return total, level + math.ceil(math.log2(parts))


def sum_over_lines(total, level, each):
    quads = lax.axis_size("sp") // 4
    message = coded(total, level, each)
    others = {k: swapped(message, 4 * k) for k in range(1, quads)}
    terms = [decoded(message, each)] + [decoded(others[k], each) for k in range(1, quads)]
    while len(terms) > 1:
        terms = [
            (left[0] + right[0], jnp.maximum(left[1], right[1]) + 1.0)
            for left, right in zip(terms[::2], terms[1::2])
        ]
    return terms[0]


def spread_over_plane(total, level, each, parts):
    message = coded(total, level, each)
    slots = {k: swapped_in_plane(message, k) for k in partners(parts)}
    slots[0] = message
    return [slots[k] for k in range(parts)]


def call(body, outs, operands, scratch=(), flops=1_000_000, spaces=None):
    vmem = pl.BlockSpec(memory_space=pltpu.VMEM)
    return pl.pallas_call(
        body,
        out_shape=outs,
        in_specs=[
            pl.BlockSpec(memory_space=(spaces or {}).get(k, pltpu.VMEM))
            for k in range(len(operands))
        ],
        out_specs=jax.tree.map(lambda _: vmem, outs),
        scratch_shapes=scratch,
        compiler_params=pltpu.CompilerParams(vmem_limit_bytes=32 * 1024 * 1024),
        cost_estimate=pl.CostEstimate(flops=flops, bytes_accessed=4_000_000, transcendentals=0),
    )(*operands)


def per_device(volume, weight, cotangent):
    channels, z_cells, y_cells, x_cells = volume.shape
    slabs, pencils = lax.axis_size("sp"), lax.axis_size("gz")
    width = channels // GROUPS
    out_channels = weight.shape[4]
    out_z, out_y, out_x = cotangent.shape[1:]
    lines = z_cells * y_cells
    cells = out_y * out_x
    out_cells = slabs * pencils * out_z * out_y * out_x
    parts = 2 * pencils
    rows = 27 * width
    each = rows // 2 // parts
    padded = (each + 8) // 8 * 8
    shape = jax.ShapeDtypeStruct

    up_z = shifted(cotangent, -1, 0)
    up_c = shifted(cotangent, -1, -1)
    up_y = shifted(cotangent, 0, -1)
    classes, own, near = call(
        lay_out_body,
        (
            shape((8, channels, cells), BF),
            shape((out_y, channels, x_cells), BF),
            shape((len(near_taps()) * width, out_channels), F32),
        ),
        (volume, cotangent),
        [],
        0,
    )
    share = shape((parts, padded, out_channels), F32)
    cots, keep, send = call(
        kernel_grad_body,
        (shape((2 * (out_y + 1), channels, x_cells), BF), share, share),
        (classes, own, near, up_z, up_y, up_c),
        [pltpu.VMEM((8, channels, cells), BF), pltpu.VMEM((rows, out_channels), F32)],
        500000000,
    )
    plane, send = in_order(classes[4:], send)
    from_z = shifted(plane, 1, 0)
    got = swapped(send, 1)
    weights = weight.reshape(27, width, out_channels)
    spread = pltpu.VMEM((27 * channels, out_channels), BF)
    volume_grad = call(
        backward_body,
        shape(volume.shape, BF),
        (cots, weights),
        [
            spread,
            pltpu.VMEM((8, channels, cells), BF),
            pltpu.VMEM((lines, channels, x_cells), BF),
        ],
        1_000_000_000,
    )
    total, level = sum_over_plane(keep, got, each, parts)
    total, volume_grad = in_order(total, volume_grad)
    total, from_z = in_order(total, from_z)
    edge = jnp.concatenate([from_z[2:], classes[2:4], classes[6:]], axis=0)[:, :, cells - out_x :]
    from_y = shifted(edge, 0, 1)
    total, level = sum_over_lines(total, level, each)
    mine = spread_over_plane(total, level, each, parts)
    output = call(
        forward_body,
        shape(cotangent.shape, BF),
        (classes, from_z, from_y, weights),
        [spread, pltpu.VMEM((27 * channels, cells), BF)],
        1_000_000_000,
    )
    mine, output = in_order(mine, output)
    other = swapped(jnp.stack(mine), 1)
    kernel_grad = None
    for side, half in enumerate((mine, other)):
        slots = [slot.astype(F32) for slot in half]
        kernel_grad = pl.pallas_call(
            functools.partial(assemble_body, 1.0 / math.sqrt(out_cells), side, parts, each),
            out_shape=shape((rows, out_channels), F32),
            in_specs=[pl.BlockSpec(memory_space=pltpu.VMEM)] * parts
            + [pl.BlockSpec(memory_space=pl.ANY)] * side,
            out_specs=pl.BlockSpec(memory_space=pl.ANY),
            scratch_shapes=[
                pltpu.VMEM((parts, each, out_channels), F32),
                pltpu.VMEM((rows // 2, out_channels), F32),
                pltpu.SemaphoreType.DMA((parts,)),
            ],
            input_output_aliases={parts: 0} if side else {},
            compiler_params=pltpu.CompilerParams(vmem_limit_bytes=32 * 1024 * 1024),
            cost_estimate=pl.CostEstimate(flops=1_000_000, bytes_accessed=1_000_000, transcendentals=0),
        )(*slots, *([kernel_grad] * side))
    kernel_grad = kernel_grad.reshape(weight.shape)
    return (output, volume_grad, kernel_grad)


def solution(mesh):
    in_specs = (P(None, "sp", "gz", None), P(), P(None, "sp", "gz", None))
    out_specs = (P(None, "sp", "gz", None), P(None, "sp", "gz", None), P())
    return jax.shard_map(
        per_device, mesh=mesh, in_specs=in_specs, out_specs=out_specs, check_vma=False
    )
```
